256 devices in a mesh: comp: 16 (over y, z_lo, core), space: 16 (over x, z_hi).
Axes of the slice: x: 4, y: 4, z: 8 (z_hi: 4, z_lo: 2; z = z_hi * 2 + z_lo), core: 2. Of those that a mesh axis runs over, the one named last changes fastest.
Arguments:
- adjoint_forcing: float32 [384, 512, 1024], P('comp', 'space'), may hold values from -6 to 6
- forward_state: bfloat16 [384, 512, 1024], P(None, ('space', 'comp')), may hold values from -6 to 6
- wind_speed: float32 [512, 1024], P(('space', 'comp')), may hold values from 0.5 to 2
- cg_index: int32 [16, 512, 1024], P('comp', 'space'), may hold values from 0 to 7
- turn_index: int32 [16, 512, 1024], P('comp', 'space'), may hold values from 0 to 7
- sea_mask: int32 [512, 1024], P('space'), may hold values 0 or 1
- dir_sign: int32 [2, 24], replicated, may hold values from -1 to 1, as said below
- w_in: bfloat16 [1536, 384], replicated, may hold values from -0.3125 to 0.3125
- w_out: bfloat16 [384, 1536], replicated, may hold values from -0.15625 to 0.15625
- wind_weight: float32 [1536], replicated, may hold values from -6 to 6
Outputs:
- adjoint_start: float32 [384, 512, 1024], P('comp', 'space')
- wind_gradient: float32 [512, 1024], P(('space', 'comp'))
The draws below stay inside these ranges and needn't reach their ends.
Inputs may be any that keep to these rules, and one draw needn't show every extreme that they name: `dir_sign`: every entry is -1 or 1.
All inputs are finite; a program needn't handle non-finite values. No bound on the sum of `sea_mask` on one device may be relied on, other than what follows from the above.
Results may differ from the reference program's by a relative error of at most 0.0035.
Values may be sent and summed in bfloat16 or wider, within the bound.
A program may use at most 64 MiB of HBM per device.

```python
import math
import jax
import jax.numpy as jnp
from jax import lax

DIRS = 24
FREQ = 16
HID = 1536
STEPS = 2
NLON = 1024
COMPONENTS = 384
NLAT = 512


def draw_dir_sign(key, part):
    key = jax.random.fold_in(key, 11)
    flips = jax.random.randint(key, (2, DIRS), 0, 2)
    return (flips * 2 - 1).astype(jnp.int32)


def set_ends(drawn, own_key, least, top_value):
    spot = [jax.random.randint(jax.random.fold_in(own_key, axis), (), 0, length) for axis, length in enumerate(drawn.shape)]
    main_axis = drawn.shape.index(max(drawn.shape))
    next_to = spot[:main_axis] + [(spot[main_axis] + 1) % drawn.shape[main_axis]] + spot[main_axis + 1:]
    return drawn.at[tuple(spot)].set(least).at[tuple(next_to)].set(top_value)


def block_scale(key, extent, shards, smallest, high):
    factor_of = 1.0
    for position, shards_of in shards:
        steps = jax.random.uniform(jax.random.fold_in(jax.random.fold_in(key, 6), position), (shards_of,), jnp.float32, smallest / len(shards), high / len(shards))
        factor_of = factor_of * jnp.repeat(jnp.exp(steps), extent[position] // shards_of).reshape((-1,) + (1,) * (len(extent) - 1 - position))
    return factor_of


def normal_values(own_key, extent, scale, most, split=(), kind=jnp.bfloat16):
    entries = scale * jax.random.normal(own_key, extent, jnp.float32)
    if split:
        entries = entries * block_scale(own_key, extent, split, -0.22, 0.18)
    return jnp.clip(entries, -most, most).astype(kind)


def setup_inputs(seed: int = 0) -> dict:
    keys = jax.random.split(jax.random.key(seed), 11)
    return {
        "adjoint_forcing": normal_values(keys[0], (COMPONENTS, NLAT, NLON), 1.0, 6.0, ((0, 16), (1, 16)), jnp.float32),
        "forward_state": normal_values(keys[1], (COMPONENTS, NLAT, NLON), 1.0, 6.0, ((1, 256),)),
        "wind_speed": jnp.clip(0.5 + 1.5 * jax.random.uniform(keys[2], (NLAT, NLON), jnp.float32) ** block_scale(keys[2], (NLAT, NLON), ((0, 256),), -0.2, 0.2), 0.5, 2.0),
        "cg_index": set_ends(jax.random.randint(keys[3], (FREQ, NLAT, NLON), 0, 8), jax.random.fold_in(keys[3], 1), 0, 7).astype(jnp.int32),
        "turn_index": set_ends(jax.random.randint(keys[4], (FREQ, NLAT, NLON), 0, 8), jax.random.fold_in(keys[4], 1), 0, 7).astype(jnp.int32),
        "sea_mask": set_ends((jax.random.randint(keys[5], (NLAT, NLON), 0, 8) < 7).astype(jnp.int32), jax.random.fold_in(keys[5], 1), 0, 1),
        "dir_sign": draw_dir_sign(jax.random.fold_in(keys[10], 71), 0),
        "w_in": normal_values(keys[7], (HID, COMPONENTS), COMPONENTS ** -0.5, 0.3125),
        "w_out": normal_values(keys[8], (COMPONENTS, HID), HID ** -0.5, 0.15625),
        "wind_weight": normal_values(keys[9], (HID,), 1.0, 6.0, (), jnp.float32),
    }


def direction_factors(dirs):
    angle = (jnp.arange(dirs, dtype=jnp.float32) + 0.5) * (2.0 * math.pi / dirs)
    return 0.5 * jnp.abs(jnp.cos(angle)), 0.5 * jnp.abs(jnp.sin(angle))


def adjoint_step(costate, celerity, turning, turn_up, sea_land, sign_x, sign_y, along_x, along_y):
    cour_x = along_x * celerity
    cour_y = along_y * celerity
    masked = costate * sea_land
    retained = (1.0 - cour_x - cour_y - turning) * masked
    flux_x = cour_x * masked
    flux_y = cour_y * masked
    flux_t = turning * masked
    zero_col = jnp.zeros_like(flux_x[..., :1])
    from_right = jnp.concatenate([flux_x[..., 1:], zero_col], axis=-1)
    from_left = jnp.concatenate([zero_col, flux_x[..., :-1]], axis=-1)
    term_x = jnp.where(sign_x > 0, from_right, from_left)
    padded = jnp.pad(flux_y, ((0, 0), (1, 1), (0, 0)))
    term_y = jnp.where(sign_y > 0, padded[:, 2:, :], padded[:, :-2, :])
    term_t = jnp.where(turn_up, jnp.roll(flux_t, -1, axis=-3), jnp.roll(flux_t, 1, axis=-3))
    return retained + term_x + term_y + term_t


def source_adjoint(cell_half, cell_state, cell_wind, w_in, w_out, wind_weight):
    pulled = jnp.dot(w_out.T, cell_half, preferred_element_type=jnp.float32)
    forward = jnp.dot(w_in, cell_state, preferred_element_type=jnp.float32) + wind_weight[:, None] * cell_wind[None, :]
    squash = jnp.tanh(forward)
    weighted = (1.0 - squash * squash) * pulled
    increment = jnp.dot(w_in.T, weighted.astype(jnp.bfloat16), preferred_element_type=jnp.float32).astype(jnp.bfloat16)
    wind_grad = jnp.sum(wind_weight[:, None] * weighted, axis=0)
    return increment, wind_grad


def reference(adjoint_forcing, forward_state, wind_speed, cg_index, turn_index, sea_mask, dir_sign, w_in, w_out, wind_weight):
    along_x, along_y = direction_factors(DIRS)
    along_x = along_x.reshape(DIRS, 1, 1)
    along_y = along_y.reshape(DIRS, 1, 1)
    sign_x = dir_sign[0].reshape(DIRS, 1, 1)
    sign_y = dir_sign[1].reshape(DIRS, 1, 1)
    sea_land = sea_mask.astype(jnp.float32)

    def propagate(pieces):
        costate, grid_index, turn_grid = pieces
        celerity = (0.1 + 0.8 * grid_index.astype(jnp.float32) / 7.0)[None]
        turning = (0.3 * jnp.abs(turn_grid.astype(jnp.float32) - 3.5) / 3.5)[None]
        turn_up = (turn_grid >= 4)[None]
        for sweep in range(STEPS):
            costate = adjoint_step(costate, celerity, turning, turn_up, sea_land, sign_x, sign_y, along_x, along_y)
        return costate

    costate = lax.map(propagate, (adjoint_forcing.reshape(FREQ, DIRS, NLAT, NLON), cg_index, turn_index))
    costate = costate.reshape(COMPONENTS, NLAT, NLON)
    cell_costate = jnp.moveaxis(costate, 1, 0)
    cell_state = jnp.moveaxis(forward_state, 1, 0)

    def source_row(pieces):
        row_costate, row_state, row_wind = pieces
        increment, wind_grad = source_adjoint(row_costate.astype(jnp.bfloat16), row_state, row_wind, w_in, w_out, wind_weight)
        return row_costate + increment.astype(jnp.float32), wind_grad

    start_rows, wind_gradient = lax.map(source_row, (cell_costate, cell_state, wind_speed))
    return jnp.moveaxis(start_rows, 0, 1), wind_gradient
```

```python
import functools
import math

import jax
import jax.numpy as jnp
import numpy as np
from jax import lax
from jax.experimental import pallas as pl
from jax.experimental.pallas import tpu as pltpu
from jax.sharding import PartitionSpec as P

MESH = pl.DeviceIdType.MESH
DIRS = 24
LANES = 128
ROWS = 32
RING = 40
TILES = 8
CHUNKS = 4
PER = TILES // CHUNKS
WIDE = PER * LANES
HID = 1536
BLOCK = 256
COMPS = 384
F32 = jnp.float32
BF16 = jnp.bfloat16


def iota(shape, dim):
    return lax.broadcasted_iota(jnp.int32, shape, dim)


def picks(mask):
    return jnp.where(mask, 1.0, 0.0).astype(BF16)


def decode(code):
    mask = jnp.where(code >= 64.0, 1.0, 0.0)
    rest = code - 64.0 * mask
    turn = jnp.floor(rest * 0.125)
    group = rest - 8.0 * turn
    celerity = 0.1 + 0.8 * group / 7.0
    turning = 0.3 * jnp.abs(turn - 3.5) / 3.5
    return mask, celerity * mask, turning * mask, turn


def kernel(
    n, slabs,
    forcing, fs, w_in_hbm, w_out_hbm, wind, cg, turn, sea, ww, sign, along,
    out, wgrad,
    C4, D4, Q0, Q1, CM, TM, MK, TN,
    HS, HR, MS, MR, S, R, IS, IR,
    FS, w_in, w_out, E, WT, A, G, WH, WW, WG,
    load_sem, w_sem, hs_sem, hr_sem, ms_sem, mr_sem, s1, r1, s2, r2, out_sem,
):
    me = lax.axis_index("comp")
    slab = lax.axis_index("space")
    C = C4.reshape(TILES, DIRS * RING, LANES)
    D = D4.reshape(TILES, DIRS * RING, LANES)
    FS2 = FS.reshape(2 * COMPS, TILES * LANES)

    def load(t):
        return pltpu.make_async_copy(
            forcing.at[:, :, pl.ds(t * LANES, LANES)], C4.at[t, :, pl.ds(0, ROWS), :], load_sem.at[t]
        )

    for t in range(TILES):
        load(t).start()
    weights = [
        pltpu.make_async_copy(fs, FS, w_sem.at[0]),
        pltpu.make_async_copy(w_in_hbm, w_in, w_sem.at[1]),
        pltpu.make_async_copy(w_out_hbm, w_out, w_sem.at[2]),
    ]
    for copy in weights:
        copy.start()

    barrier = pltpu.get_barrier_semaphore()

    def greet(step, carry):
        pl.semaphore_signal(
            barrier, inc=1, device_id={"comp": lax.rem(me + step, n)}, device_id_type=MESH
        )
        return carry

    lax.fori_loop(1, n, greet, 0)
    has_prev = slab > 0
    has_next = slab < slabs - 1

    @pl.when(has_prev)
    def _():
        pl.semaphore_signal(barrier, inc=1, device_id={"space": slab - 1}, device_id_type=MESH)

    @pl.when(has_next)
    def _():
        pl.semaphore_signal(barrier, inc=1, device_id={"space": slab + 1}, device_id_type=MESH)

    def code_of(rows):
        return (cg[0, rows, :] + 8 * turn[0, rows, :] + 64 * sea[rows, :]).astype(F32)

    MS[0] = code_of(slice(0, 2))
    MS[1] = code_of(slice(ROWS - 2, ROWS))

    def packed(t, row):
        first = C[t, pl.ds(row, DIRS, stride=RING), :]
        second = C[t, pl.ds(row + 1, DIRS, stride=RING), :]
        mixed = jnp.concatenate([first[16:], second[16:]], axis=0)
        return first[:16].astype(BF16), second[:16].astype(BF16), mixed.astype(BF16)

    def halo_copies(h, side):
        peer = slab - 1 if side == 0 else slab + 1
        return pltpu.make_async_remote_copy(
            src_ref=HS.at[h, side], dst_ref=HR.at[h, 1 - side],
            send_sem=hs_sem.at[h, side], recv_sem=hr_sem.at[h, 1 - side],
            device_id={"space": peer}, device_id_type=MESH,
        )

    def meta_copies(side):
        peer = slab - 1 if side == 0 else slab + 1
        return pltpu.make_async_remote_copy(
            src_ref=MS.at[side], dst_ref=MR.at[1 - side],
            send_sem=ms_sem.at[side], recv_sem=mr_sem.at[1 - side],
            device_id={"space": peer}, device_id_type=MESH,
        )

    def halo_arrived(h, side):
        peer = slab - 1 if side == 0 else slab + 1
        return pltpu.make_async_remote_copy(
            src_ref=HS.at[h, side], dst_ref=HR.at[h, side],
            send_sem=hs_sem.at[h, side], recv_sem=hr_sem.at[h, side],
            device_id={"space": peer}, device_id_type=MESH,
        )

    def meta_arrived(side):
        peer = slab - 1 if side == 0 else slab + 1
        return pltpu.make_async_remote_copy(
            src_ref=MS.at[side], dst_ref=MR.at[side],
            send_sem=ms_sem.at[side], recv_sem=mr_sem.at[side],
            device_id={"space": peer}, device_id_type=MESH,
        )

    for h in range(CHUNKS):
        for k in range(PER):
            t = h * PER + k
            load(t).wait()
            lanes = pl.ds(k * LANES, LANES)
            for side, row in ((0, 0), (1, ROWS - 2)):
                for part, value in enumerate(packed(t, row)):
                    HS[h, side, part, :, lanes] = value
        if h == 0:
            pl.semaphore_wait(barrier, n - 1 + has_prev.astype(jnp.int32) + has_next.astype(jnp.int32))
        for side, there in ((0, has_prev), (1, has_next)):

            @pl.when(there)
            def _(side=side, h=h):
                if h == 0:
                    meta_copies(side).start()
                halo_copies(h, side).start()

    for side, there in ((0, has_prev), (1, has_next)):

        @pl.when(jnp.logical_not(there))
        def _(side=side):
            MR[side] = jnp.zeros((2, TILES * LANES), F32)
            HR[:, side] = jnp.zeros((CHUNKS, 3, 16, WIDE), BF16)

    def levels(t, rows, code):
        mask, flow, turns, level = decode(code)
        MK[t, rows, :] = mask
        CM[t, rows, :] = flow
        TM[t, rows, :] = turns
        TN[t, rows, :] = level

    for t in range(TILES):
        lanes = slice(t * LANES, (t + 1) * LANES)
        code = (cg[0, :, lanes] + 8 * turn[0, :, lanes] + 64 * sea[:, lanes]).astype(F32)
        levels(t, slice(0, ROWS), code)

    def clear(d, carry):
        rows = pl.ds(pl.multiple_of(d * RING, 8), RING)
        zero = jnp.zeros((RING, LANES), F32)
        for q in (Q0, Q1):
            q[0, rows, :] = zero
            q[TILES + 1, rows, :] = zero
        return carry

    lax.fori_loop(0, DIRS, clear, 0)

    def weigh(t, carry):
        flow = CM[t, 0:ROWS, :]

        def one(d, carry):
            rows = pl.ds(pl.multiple_of(d * RING, 8), ROWS)
            Q0[t + 1, rows, :] = flow * C[t, rows, :]
            return carry

        return lax.fori_loop(0, DIRS, one, carry, unroll=4)

    lax.fori_loop(0, TILES, weigh, 0)

    for side, there in ((0, has_prev), (1, has_next)):

        @pl.when(there)
        def _(side=side):
            meta_arrived(side).wait_recv()

    for t in range(TILES):
        lanes = slice(t * LANES, (t + 1) * LANES)
        blank = jnp.zeros((4, LANES), F32)
        code = jnp.concatenate([MR[1, :, lanes], blank, MR[0, :, lanes]], axis=0)
        levels(t, slice(ROWS, RING), code)

    def take_halo(h):
        for side, there in ((0, has_prev), (1, has_next)):

            @pl.when(there)
            def _(side=side):
                halo_arrived(h, side).wait_recv()

        for k in range(PER):
            t = h * PER + k
            lanes = pl.ds(k * LANES, LANES)
            for side, row in ((0, RING - 2), (1, ROWS)):
                parts = [HR[h, side, part, :, lanes].astype(F32) for part in range(3)]
                for i in range(2):
                    value = jnp.concatenate([parts[i], parts[2][8 * i : 8 * i + 8]], axis=0)
                    C[t, pl.ds(row + i, DIRS, stride=RING), :] = value
            zero = jnp.zeros((DIRS, LANES), F32)
            for i in range(ROWS + 2, RING - 2):
                C[t, pl.ds(i, DIRS, stride=RING), :] = zero
            flow = CM[t, ROWS:RING, :]

            def one(d, carry):
                rows = pl.ds(pl.multiple_of(d * RING + ROWS, 8), RING - ROWS)
                Q0[t + 1, rows, :] = flow * C[t, rows, :]
                return carry

            lax.fori_loop(0, DIRS, one, 0, unroll=4)

    lane = iota((RING, LANES), 1)
    at_first = lane == 0
    at_last = lane == LANES - 1

    def step(t, state, q, result, next_q):
        flow = CM[t]
        turns = TM[t]
        mask = MK[t]
        up = TN[t] >= 4.0

        def one(d, carry):
            rows = pl.ds(pl.multiple_of(d * RING, 8), RING)
            above = pl.ds(pl.multiple_of(lax.rem(d + 1, DIRS) * RING, 8), RING)
            below = pl.ds(pl.multiple_of(lax.rem(d + DIRS - 1, DIRS) * RING, 8), RING)
            ax, ay = along[0, d], along[1, d]
            right = ax * (0.5 + 0.5 * sign[0, d].astype(F32))
            left = ax - right
            north = ay * (0.5 + 0.5 * sign[1, d].astype(F32))
            south = ay - north
            c = state[t, rows, :]
            here = q[t + 1, rows, :]
            from_right = pltpu.roll(jnp.where(at_first, q[t + 2, rows, :], here), LANES - 1, 1)
            from_left = pltpu.roll(jnp.where(at_last, q[t, rows, :], here), 1, 1)
            from_north = pltpu.roll(here, RING - 1, 0)
            from_south = pltpu.roll(here, 1, 0)
            turned = turns * (jnp.where(up, state[t, above, :], state[t, below, :]) - c)
            new = (
                mask * c
                + turned
                + (right * from_right + left * from_left)
                + (north * from_north + south * from_south)
                - (ax + ay) * here
            )
            if next_q is None:
                result[t, pl.ds(pl.multiple_of(d * RING, 8), ROWS), :] = new[:ROWS]
            else:
                result[t, rows, :] = new
                next_q[t + 1, rows, :] = flow * new
            return carry

        lax.fori_loop(0, DIRS, one, 0, unroll=4)

    def first_step(t, carry):
        step(t, C, Q0, D, Q1)
        return carry

    def second_step(t, carry):
        step(t, D, Q1, C, None)
        return carry

    def rows_of(p):
        return pl.ds(pl.multiple_of(p * 16, 16), 16)

    def exchange(h, p, source, target, send, recv):
        return pltpu.make_async_remote_copy(
            src_ref=source.at[h, :, rows_of(p), :], dst_ref=target.at[h, :, rows_of(me), :],
            send_sem=send.at[h, p], recv_sem=recv.at[h, me],
            device_id={"comp": p}, device_id_type=MESH,
        )

    def arrival(h, p, source, target, send, recv):
        return pltpu.make_async_remote_copy(
            src_ref=source.at[h, :, rows_of(me), :], dst_ref=target.at[h, :, rows_of(p), :],
            send_sem=send.at[h, p], recv_sem=recv.at[h, p],
            device_id={"comp": p}, device_id_type=MESH,
        )

    def own(h, source, target, recv):
        return pltpu.make_async_copy(
            source.at[h, :, rows_of(me), :], target.at[h, :, rows_of(me), :], recv.at[h, me]
        )

    def pack_for(h, p):
        for k in range(PER):
            lanes = pl.ds(k * LANES, LANES)
            for part, value in enumerate(packed(h * PER + k, 2 * p)):
                S[h, part, rows_of(p), lanes] = value

    take_halo(0)
    first_step(0, 0)

    def propagate(h, carry):
        @pl.when(h < CHUNKS - 1)
        def _():
            take_halo(h + 1)

        lax.fori_loop(h * PER + 1, jnp.minimum(h * PER + PER + 1, TILES), first_step, 0)
        lax.fori_loop(h * PER, h * PER + PER, second_step, 0)

        def send(i, carry):
            p = lax.rem(me + i, n)
            pack_for(h, p)
            exchange(h, p, S, R, s1, r1).start()
            return carry

        lax.fori_loop(1, n, send, 0)
        pack_for(h, me)
        own(h, S, R, r1).start()
        return carry

    lax.fori_loop(0, CHUNKS, propagate, 0)

    for copy in weights:
        copy.wait()
    wide = (COMPS, 2 * COMPS)
    for r in range(2):
        E[r] = picks(iota(wide, 1) == 2 * iota(wide, 0) + r)

    square = (COMPS, COMPS)
    place = iota(square, 0)
    rest = place - 256
    comp = jnp.where(
        place < 256,
        24 * lax.shift_right_logical(place, 4) + (place & 15),
        24 * lax.shift_right_arithmetic(rest, 3) + 16 + (rest & 7),
    )
    order = picks(iota(square, 1) == comp)
    nt = (((1,), (1,)), ((), ()))
    for m in range(HID // BLOCK):
        A[:, m * BLOCK : (m + 1) * BLOCK] = lax.dot_general(
            order, w_in[m * BLOCK : (m + 1) * BLOCK, :], nt, preferred_element_type=F32
        ).astype(BF16)

    tall = (COMPS, 512)
    place = iota(tall, 1)
    within = place & 15
    base = 24 * lax.shift_right_logical(place & 255, 4)
    eye = picks(iota((BLOCK, BLOCK), 0) == iota((BLOCK, BLOCK), 1))
    for r in range(2):
        mixed = jnp.where(
            lax.shift_right_logical(within, 3) == r, base + 16 + (within & 7), -1
        )
        chosen = picks(iota(tall, 0) == jnp.where(place < 256, base + within, mixed))
        for m in range(HID // BLOCK):
            turned = lax.dot_general(
                eye, w_out[:, m * BLOCK : (m + 1) * BLOCK], nt, preferred_element_type=F32
            ).astype(BF16)
            WT[r, m * BLOCK : (m + 1) * BLOCK, :] = jnp.dot(
                turned, chosen, preferred_element_type=F32
            ).astype(BF16)

    for b in range(HID // LANES):
        row = ww[0:1, b * LANES : (b + 1) * LANES]
        WW[b * LANES : (b + 1) * LANES, :] = jnp.broadcast_to(row, (LANES, LANES)).T

    def block_rows(m):
        return pl.ds(pl.multiple_of(m * BLOCK, BLOCK), BLOCK)

    def slopes(m, carry):
        rows = block_rows(m)
        winds = jnp.concatenate([WW[rows, :]] * PER, axis=1)
        for r in range(2):
            spread = jnp.dot(w_in[rows, :], E[r], preferred_element_type=F32).astype(BF16)
            for h in range(CHUNKS):
                lanes = slice(h * WIDE, (h + 1) * WIDE)
                squash = jnp.tanh(
                    jnp.dot(spread, FS2[:, lanes], preferred_element_type=F32)
                    + winds * wind[r : r + 1, lanes]
                )
                G[h, r, rows, :] = 1.0 - squash * squash
        return carry

    lax.fori_loop(0, HID // BLOCK, slopes, 0)

    def arrived(h, source, target, send, recv):
        def one(i, carry):
            arrival(h, lax.rem(me + n - i, n), source, target, send, recv).wait_recv()
            return carry

        lax.fori_loop(1, n, one, 0)
        own(h, source, target, recv).wait()

    def network(h, carry):
        arrived(h, S, R, s1, r1)
        tails = []
        for r in range(2):
            cells = jnp.concatenate([R[h, r], R[h, 2]], axis=0)

            def block(m, total):
                rows = block_rows(m)
                pulled = jnp.dot(WT[r, rows, :], cells, preferred_element_type=F32)
                weighted = G[h, r, rows, :] * pulled
                WH[rows, :] = weighted.astype(BF16)
                winds = jnp.concatenate([WW[rows, :]] * PER, axis=1)
                return total + jnp.sum((winds * weighted).reshape(BLOCK // 8, 8, WIDE), axis=0)

            total = lax.fori_loop(0, HID // BLOCK, block, jnp.zeros((8, WIDE), F32))
            WG[h, r : r + 1, :] = jnp.sum(total, axis=0, keepdims=True)
            increment = jnp.dot(A[...], WH[...], preferred_element_type=F32)
            IS[h, r] = increment[:256].astype(BF16)
            tails.append(increment[256:].reshape(16, 1, 8, WIDE))
        IS[h, 2] = jnp.concatenate(tails, axis=1).reshape(256, WIDE).astype(BF16)

        def send(i, carry):
            exchange(h, lax.rem(me + i, n), IS, IR, s2, r2).start()
            return carry

        lax.fori_loop(1, n, send, 0)
        own(h, IS, IR, r2).start()
        return carry

    lax.fori_loop(0, CHUNKS, network, 0)

    for h in range(CHUNKS):
        wgrad[:, h * WIDE : (h + 1) * WIDE] = WG[h]

    def store(t):
        return pltpu.make_async_copy(
            C4.at[t, :, pl.ds(0, ROWS), :], out.at[:, :, pl.ds(t * LANES, LANES)], out_sem.at[t]
        )

    for h in range(CHUNKS):
        arrived(h, IS, IR, s2, r2)

        def add(p, carry):
            for k in range(PER):
                lanes = pl.ds(k * LANES, LANES)
                parts = [IR[h, part, rows_of(p), lanes].astype(F32) for part in range(3)]
                for r in range(2):
                    value = jnp.concatenate([parts[r], parts[2][8 * r : 8 * r + 8]], axis=0)
                    rows = pl.ds(2 * p + r, DIRS, stride=RING)
                    C[h * PER + k, rows, :] = C[h * PER + k, rows, :] + value
            return carry

        lax.fori_loop(0, n, add, 0)
        for k in range(PER):
            store(h * PER + k).start()

    for t in range(TILES):
        store(t).wait()

    def sent(i, carry):
        p = lax.rem(me + i, n)
        for h in range(CHUNKS):
            exchange(h, p, S, R, s1, r1).wait_send()
            exchange(h, p, IS, IR, s2, r2).wait_send()
        return carry

    lax.fori_loop(1, n, sent, 0)
    for side, there in ((0, has_prev), (1, has_next)):

        @pl.when(there)
        def _(side=side):
            meta_copies(side).wait_send()
            for h in range(CHUNKS):
                halo_copies(h, side).wait_send()


def shards(n, slabs, forcing, state, wind, cg, turn, sea, sign, w_in, w_out, ww):
    angle = (np.arange(DIRS) + 0.5) * (2.0 * math.pi / DIRS)
    along = jnp.asarray(
        np.stack([0.5 * np.abs(np.cos(angle)), 0.5 * np.abs(np.sin(angle))]).astype(np.float32)
    )
    hbm = pl.BlockSpec(memory_space=pl.ANY)
    vmem = pl.BlockSpec(memory_space=pltpu.VMEM)
    smem = pl.BlockSpec(memory_space=pltpu.SMEM)
    sems = pltpu.SemaphoreType.DMA
    field = (TILES, DIRS, RING, LANES)
    fluxes = (TILES + 2, DIRS * RING, LANES)
    cells = (TILES, RING, LANES)
    message = (CHUNKS, 3, 16 * n, WIDE)
    return pl.pallas_call(
        functools.partial(kernel, n, slabs),
        out_shape=(
            jax.ShapeDtypeStruct(forcing.shape, F32),
            jax.ShapeDtypeStruct(wind.shape, F32),
        ),
        in_specs=[hbm] * 4 + [vmem] * 5 + [smem] * 2,
        out_specs=(hbm, vmem),
        scratch_shapes=[
            pltpu.VMEM(field, F32),
            pltpu.VMEM(field, F32),
            pltpu.VMEM(fluxes, F32),
            pltpu.VMEM(fluxes, F32),
            pltpu.VMEM(cells, F32),
            pltpu.VMEM(cells, F32),
            pltpu.VMEM(cells, F32),
            pltpu.VMEM(cells, F32),
            pltpu.VMEM((CHUNKS, 2, 3, 16, WIDE), BF16),
            pltpu.VMEM((CHUNKS, 2, 3, 16, WIDE), BF16),
            pltpu.VMEM((2, 2, TILES * LANES), F32),
            pltpu.VMEM((2, 2, TILES * LANES), F32),
            pltpu.VMEM(message, BF16),
            pltpu.VMEM(message, BF16),
            pltpu.VMEM(message, BF16),
            pltpu.VMEM(message, BF16),
            pltpu.VMEM(state.shape, BF16),
            pltpu.VMEM(w_in.shape, BF16),
            pltpu.VMEM(w_out.shape, BF16),
            pltpu.VMEM((2, COMPS, 2 * COMPS), BF16),
            pltpu.VMEM((2, HID, 512), BF16),
            pltpu.VMEM((COMPS, HID), BF16),
            pltpu.VMEM((CHUNKS, 2, HID, WIDE), F32),
            pltpu.VMEM((HID, WIDE), BF16),
            pltpu.VMEM((HID, LANES), F32),
            pltpu.VMEM((CHUNKS, 2, WIDE), F32),
            sems((TILES,)),
            sems((3,)),
            sems((CHUNKS, 2)),
            sems((CHUNKS, 2)),
            sems((2,)),
            sems((2,)),
            sems((CHUNKS, n)),
            sems((CHUNKS, n)),
            sems((CHUNKS, n)),
            sems((CHUNKS, n)),
            sems((TILES,)),
        ],
        compiler_params=pltpu.CompilerParams(
            collective_id=0, has_side_effects=True, vmem_limit_bytes=58 << 20
        ),
        name="adjoint_window",
    )(forcing, state, w_in, w_out, wind, cg, turn, sea, ww.reshape(1, -1), sign, along)


def solution(mesh):
    placed = (
        P("comp", "space", None),
        P(None, ("space", "comp"), None),
        P(("space", "comp"), None),
        P("comp", "space", None),
        P("comp", "space", None),
        P("space", None),
        P(),
        P(),
        P(),
        P(),
    )
    return jax.shard_map(
        functools.partial(shards, mesh.shape["comp"], mesh.shape["space"]),
        mesh=mesh,
        in_specs=placed,
        out_specs=(P("comp", "space", None), P(("space", "comp"), None)),
        check_vma=False,
    )
```

```python
import functools
import math

import jax
import jax.numpy as jnp
import numpy as np
from jax import lax
from jax.experimental import pallas as pl
from jax.experimental.pallas import tpu as pltpu
from jax.sharding import PartitionSpec as P

MESH = pl.DeviceIdType.MESH
DIRS = 24
LANES = 128
ROWS = 32
RING = 40
TILES = 8
CHUNKS = 4
PER = TILES // CHUNKS
WIDE = PER * LANES
HID = 1536
BLOCK = 256
COMPS = 384
F32 = jnp.float32
BF16 = jnp.bfloat16


def iota(shape, dim):
    return lax.broadcasted_iota(jnp.int32, shape, dim)


def picks(mask):
    return jnp.where(mask, 1.0, 0.0).astype(BF16)


def decode(code):
    mask = jnp.where(code >= 64.0, 1.0, 0.0)
    rest = code - 64.0 * mask
    turn = jnp.floor(rest * 0.125)
    group = rest - 8.0 * turn
    celerity = 0.1 + 0.8 * group / 7.0
    turning = 0.3 * jnp.abs(turn - 3.5) / 3.5
    return mask, celerity * mask, turning * mask, turn


def kernel(
    n, slabs,
    forcing, fs, w_in_hbm, w_out_hbm, cg_hbm, turn_hbm, sea_hbm, wind_hbm, ww_hbm, sign, along,
    out, wgrad,
    C4, D4, Q0, Q1, CM, TM, MK, TN,
    HS, HR, MS, MR, S, R, IS, IR,
    cg, turn, sea, wind, ww, FS4, w_in, w_out, E, WT, A, G, WH, WW, WG,
    load_sem, w_sem, hs_sem, hr_sem, ms_sem, mr_sem, s1, r1, s2, r2, out_sem,
):
    me = lax.axis_index("comp")
    slab = lax.axis_index("space")
    C = C4.reshape(TILES, DIRS * RING, LANES)
    D = D4.reshape(TILES, DIRS * RING, LANES)

    def load(t):
        return pltpu.make_async_copy(
            forcing.at[:, :, pl.ds(t * LANES, LANES)], C4.at[t, :, pl.ds(0, ROWS), :], load_sem.at[t]
        )

    for t in range(TILES):
        load(t).start()
    FS = FS4.reshape(CHUNKS, 2 * COMPS, WIDE)
    maps = [
        pltpu.make_async_copy(cg_hbm.at[0], cg, w_sem.at[2]),
        pltpu.make_async_copy(turn_hbm.at[0], turn, w_sem.at[3]),
        pltpu.make_async_copy(sea_hbm, sea, w_sem.at[4]),
    ]
    for copy in maps:
        copy.start()
    weights = [
        pltpu.make_async_copy(wind_hbm, wind, w_sem.at[5 + CHUNKS]),
        pltpu.make_async_copy(ww_hbm, ww, w_sem.at[6 + CHUNKS]),
        pltpu.make_async_copy(w_in_hbm, w_in, w_sem.at[0]),
        pltpu.make_async_copy(w_out_hbm, w_out, w_sem.at[1]),
    ] + [
        pltpu.make_async_copy(
            fs.at[:, :, pl.ds(h * WIDE, WIDE)], FS4.at[h], w_sem.at[5 + h]
        )
        for h in range(CHUNKS)
    ]
    for copy in weights:
        copy.start()

    barrier = pltpu.get_barrier_semaphore()

    def greet(step, carry):
        pl.semaphore_signal(
            barrier, inc=1, device_id={"comp": lax.rem(me + step, n)}, device_id_type=MESH
        )
        return carry

    lax.fori_loop(1, n, greet, 0)
    has_prev = slab > 0
    has_next = slab < slabs - 1

    @pl.when(has_prev)
    def _():
        pl.semaphore_signal(barrier, inc=1, device_id={"space": slab - 1}, device_id_type=MESH)

    @pl.when(has_next)
    def _():
        pl.semaphore_signal(barrier, inc=1, device_id={"space": slab + 1}, device_id_type=MESH)

    for copy in maps:
        copy.wait()

    def code_of(rows):
        return (cg[rows, :] + 8 * turn[rows, :] + 64 * sea[rows, :]).astype(F32)

    MS[0] = code_of(slice(0, 2))
    MS[1] = code_of(slice(ROWS - 2, ROWS))

    def packed(t, row):
        first = C[t, pl.ds(row, DIRS, stride=RING), :]
        second = C[t, pl.ds(row + 1, DIRS, stride=RING), :]
        mixed = jnp.concatenate([first[16:], second[16:]], axis=0)
        return first[:16].astype(BF16), second[:16].astype(BF16), mixed.astype(BF16)

    def halo_copies(h, side):
        peer = slab - 1 if side == 0 else slab + 1
        return pltpu.make_async_remote_copy(
            src_ref=HS.at[h, side], dst_ref=HR.at[h, 1 - side],
            send_sem=hs_sem.at[h, side], recv_sem=hr_sem.at[h, 1 - side],
            device_id={"space": peer}, device_id_type=MESH,
        )

    def meta_copies(side):
        peer = slab - 1 if side == 0 else slab + 1
        return pltpu.make_async_remote_copy(
            src_ref=MS.at[side], dst_ref=MR.at[1 - side],
            send_sem=ms_sem.at[side], recv_sem=mr_sem.at[1 - side],
            device_id={"space": peer}, device_id_type=MESH,
        )

    def halo_arrived(h, side):
        peer = slab - 1 if side == 0 else slab + 1
        return pltpu.make_async_remote_copy(
            src_ref=HS.at[h, side], dst_ref=HR.at[h, side],
            send_sem=hs_sem.at[h, side], recv_sem=hr_sem.at[h, side],
            device_id={"space": peer}, device_id_type=MESH,
        )

    def meta_arrived(side):
        peer = slab - 1 if side == 0 else slab + 1
        return pltpu.make_async_remote_copy(
            src_ref=MS.at[side], dst_ref=MR.at[side],
            send_sem=ms_sem.at[side], recv_sem=mr_sem.at[side],
            device_id={"space": peer}, device_id_type=MESH,
        )

    for h in range(CHUNKS):
        for k in range(PER):
            t = h * PER + k
            load(t).wait()
            lanes = pl.ds(k * LANES, LANES)
            for side, row in ((0, 0), (1, ROWS - 2)):
                for part, value in enumerate(packed(t, row)):
                    HS[h, side, part, :, lanes] = value
        if h == 0:
            pl.semaphore_wait(barrier, n - 1 + has_prev.astype(jnp.int32) + has_next.astype(jnp.int32))
        for side, there in ((0, has_prev), (1, has_next)):

            @pl.when(there)
            def _(side=side, h=h):
                if h == 0:
                    meta_copies(side).start()
                halo_copies(h, side).start()

    for side, there in ((0, has_prev), (1, has_next)):

        @pl.when(jnp.logical_not(there))
        def _(side=side):
            MR[side] = jnp.zeros((2, TILES * LANES), F32)
            HR[:, side] = jnp.zeros((CHUNKS, 3, 16, WIDE), BF16)

    def levels(t, rows, code):
        mask, flow, turns, level = decode(code)
        MK[t, rows, :] = mask
        CM[t, rows, :] = flow
        TM[t, rows, :] = turns
        TN[t, rows, :] = level

    for t in range(TILES):
        lanes = slice(t * LANES, (t + 1) * LANES)
        code = (cg[:, lanes] + 8 * turn[:, lanes] + 64 * sea[:, lanes]).astype(F32)
        levels(t, slice(0, ROWS), code)

    def clear(d, carry):
        rows = pl.ds(pl.multiple_of(d * RING, 8), RING)
        zero = jnp.zeros((RING, LANES), F32)
        for q in (Q0, Q1):
            q[0, rows, :] = zero
            q[TILES + 1, rows, :] = zero
        return carry

    lax.fori_loop(0, DIRS, clear, 0)

    def weigh(t, carry):
        flow = CM[t, 0:ROWS, :]

        def one(d, carry):
            rows = pl.ds(pl.multiple_of(d * RING, 8), ROWS)
            Q0[t + 1, rows, :] = flow * C[t, rows, :]
            return carry

        return lax.fori_loop(0, DIRS, one, carry, unroll=4)

    lax.fori_loop(0, TILES, weigh, 0)

    for side, there in ((0, has_prev), (1, has_next)):

        @pl.when(there)
        def _(side=side):
            meta_arrived(side).wait_recv()

    for t in range(TILES):
        lanes = slice(t * LANES, (t + 1) * LANES)
        blank = jnp.zeros((4, LANES), F32)
        code = jnp.concatenate([MR[1, :, lanes], blank, MR[0, :, lanes]], axis=0)
        levels(t, slice(ROWS, RING), code)

    def take_halo(h):
        for side, there in ((0, has_prev), (1, has_next)):

            @pl.when(there)
            def _(side=side):
                halo_arrived(h, side).wait_recv()

        for k in range(PER):
            t = h * PER + k
            lanes = pl.ds(k * LANES, LANES)
            for side, row in ((0, RING - 2), (1, ROWS)):
                parts = [HR[h, side, part, :, lanes].astype(F32) for part in range(3)]
                for i in range(2):
                    value = jnp.concatenate([parts[i], parts[2][8 * i : 8 * i + 8]], axis=0)
                    C[t, pl.ds(row + i, DIRS, stride=RING), :] = value
            zero = jnp.zeros((DIRS, LANES), F32)
            for i in range(ROWS + 2, RING - 2):
                C[t, pl.ds(i, DIRS, stride=RING), :] = zero
            flow = CM[t, ROWS:RING, :]

            def one(d, carry):
                rows = pl.ds(pl.multiple_of(d * RING + ROWS, 8), RING - ROWS)
                Q0[t + 1, rows, :] = flow * C[t, rows, :]
                return carry

            lax.fori_loop(0, DIRS, one, 0, unroll=4)

    lane = iota((RING, LANES), 1)

    def step(t, state, q, result, next_q):
        flow = CM[t]
        turns = TM[t]
        mask = MK[t]
        up = TN[t] >= 4.0

        def one(d, carry):
            rows = pl.ds(pl.multiple_of(d * RING, 8), RING)
            above = pl.ds(pl.multiple_of(lax.rem(d + 1, DIRS) * RING, 8), RING)
            below = pl.ds(pl.multiple_of(lax.rem(d + DIRS - 1, DIRS) * RING, 8), RING)
            ax, ay = along[0, d], along[1, d]
            toward = sign[0, d]
            north = ay * (0.5 + 0.5 * sign[1, d].astype(F32))
            south = ay - north
            c = state[t, rows, :]
            here = q[t + 1, rows, :]
            edge = jnp.where(toward > 0, 0, LANES - 1)
            shift = jnp.where(toward > 0, LANES - 1, 1)
            beside = q[t + 1 + toward, rows, :]
            from_side = pltpu.roll(jnp.where(lane == edge, beside, here), shift, 1)
            from_north = pltpu.roll(here, RING - 1, 0)
            from_south = pltpu.roll(here, 1, 0)
            turned = turns * (jnp.where(up, state[t, above, :], state[t, below, :]) - c)
            new = (
                mask * c
                + turned
                + ax * from_side
                + (north * from_north + south * from_south)
                - (ax + ay) * here
            )
            if next_q is None:
                result[t, pl.ds(pl.multiple_of(d * RING, 8), ROWS), :] = new[:ROWS]
            else:
                result[t, rows, :] = new
                next_q[t + 1, rows, :] = flow * new
            return carry

        lax.fori_loop(0, DIRS, one, 0, unroll=True)

    def first_step(t, carry):
        step(t, C, Q0, D, Q1)
        return carry

    def second_step(t, carry):
        step(t, D, Q1, C, None)
        return carry

    def rows_of(p):
        return pl.ds(pl.multiple_of(p * 16, 16), 16)

    def exchange(h, p, source, target, send, recv):
        return pltpu.make_async_remote_copy(
            src_ref=source.at[h, :, rows_of(p), :], dst_ref=target.at[h, :, rows_of(me), :],
            send_sem=send.at[h], recv_sem=recv.at[h],
            device_id={"comp": p}, device_id_type=MESH,
        )

    def all_of(h, buffer, sem):
        others = buffer.at[h, :, pl.ds(0, 16 * (n - 1)), :]
        return pltpu.make_async_copy(others, others, sem.at[h])

    def pack_for(h, p, buffer):
        for k in range(PER):
            lanes = pl.ds(k * LANES, LANES)
            for part, value in enumerate(packed(h * PER + k, 2 * p)):
                buffer[h, part, rows_of(p), lanes] = value

    take_halo(0)

    def propagate(h, carry):
        @pl.when(h < CHUNKS - 1)
        def _():
            take_halo(h + 1)

        first = jnp.where(h == 0, 0, h * PER + 1)
        lax.fori_loop(first, jnp.minimum(h * PER + PER + 1, TILES), first_step, 0)
        lax.fori_loop(h * PER, h * PER + PER, second_step, 0)

        def send(i, carry):
            p = lax.rem(me + i, n)
            pack_for(h, p, S)
            exchange(h, p, S, R, s1, r1).start()
            return carry

        lax.fori_loop(1, n, send, 0)
        pack_for(h, me, R)
        return carry

    lax.fori_loop(0, CHUNKS, propagate, 0)

    for copy in weights:
        copy.wait()
    wide = (COMPS, 2 * COMPS)
    for r in range(2):
        E[r] = picks(iota(wide, 1) == 2 * iota(wide, 0) + r)

    square = (COMPS, COMPS)
    place = iota(square, 0)
    rest = place - 256
    comp = jnp.where(
        place < 256,
        24 * lax.shift_right_logical(place, 4) + (place & 15),
        24 * lax.shift_right_arithmetic(rest, 3) + 16 + (rest & 7),
    )
    order = picks(iota(square, 1) == comp)
    nt = (((1,), (1,)), ((), ()))
    for m in range(HID // BLOCK):
        A[:, m * BLOCK : (m + 1) * BLOCK] = lax.dot_general(
            order, w_in[m * BLOCK : (m + 1) * BLOCK, :], nt, preferred_element_type=F32
        ).astype(BF16)

    tall = (COMPS, 512)
    place = iota(tall, 1)
    within = place & 15
    base = 24 * lax.shift_right_logical(place & 255, 4)
    eye = picks(iota((BLOCK, BLOCK), 0) == iota((BLOCK, BLOCK), 1))
    chosen = []
    for r in range(2):
        mixed = jnp.where(
            lax.shift_right_logical(within, 3) == r, base + 16 + (within & 7), -1
        )
        chosen.append(picks(iota(tall, 0) == jnp.where(place < 256, base + within, mixed)))
    for m in range(HID // BLOCK):
        rows = slice(m * BLOCK, (m + 1) * BLOCK)
        turned = lax.dot_general(eye, w_out[:, rows], nt, preferred_element_type=F32).astype(BF16)
        for r in range(2):
            WT[r, rows, :] = jnp.dot(turned, chosen[r], preferred_element_type=F32).astype(BF16)

    for b in range(HID // LANES):
        row = ww[b * LANES : (b + 1) * LANES].reshape(1, LANES)
        WW[b * LANES : (b + 1) * LANES, :] = jnp.broadcast_to(row, (LANES, LANES)).T

    def block_rows(m):
        return pl.ds(pl.multiple_of(m * BLOCK, BLOCK), BLOCK)

    def slopes(h):
        for r in range(2):
            cells = jnp.dot(E[r], FS[h], preferred_element_type=F32).astype(BF16)
            gusts = wind[r : r + 1, pl.ds(pl.multiple_of(h * WIDE, WIDE), WIDE)]

            def block(m, carry):
                rows = block_rows(m)
                winds = jnp.concatenate([WW[rows, :]] * PER, axis=1)
                squash = jnp.tanh(
                    jnp.dot(w_in[rows, :], cells, preferred_element_type=F32) + winds * gusts
                )
                G[r, rows, :] = 1.0 - squash * squash
                return carry

            lax.fori_loop(0, HID // BLOCK, block, 0, unroll=True)

    def network(h, carry):
        slopes(h)
        all_of(h, R, r1).wait()
        tails = []
        for r in range(2):
            cells = jnp.concatenate([R[h, r], R[h, 2]], axis=0)

            def block(m, total):
                rows = block_rows(m)
                pulled = jnp.dot(WT[r, rows, :], cells, preferred_element_type=F32)
                weighted = G[r, rows, :] * pulled
                WH[rows, :] = weighted.astype(BF16)
                winds = jnp.concatenate([WW[rows, :]] * PER, axis=1)
                return total + jnp.sum((winds * weighted).reshape(BLOCK // 8, 8, WIDE), axis=0)

            total = lax.fori_loop(
                0, HID // BLOCK, block, jnp.zeros((8, WIDE), F32), unroll=True
            )
            WG[h, r : r + 1, :] = jnp.sum(total, axis=0, keepdims=True)
            increment = jnp.dot(A[...], WH[...], preferred_element_type=F32)
            IS[h, r] = increment[:256].astype(BF16)
            tails.append(increment[256:].reshape(16, 1, 8, WIDE))
        IS[h, 2] = jnp.concatenate(tails, axis=1).reshape(256, WIDE).astype(BF16)

        def send(i, carry):
            exchange(h, lax.rem(me + i, n), IS, IR, s2, r2).start()
            return carry

        lax.fori_loop(1, n, send, 0)
        IR[h, :, rows_of(me), :] = IS[h, :, rows_of(me), :]
        return carry

    lax.fori_loop(0, CHUNKS, network, 0)

    for h in range(CHUNKS):
        wgrad[:, h * WIDE : (h + 1) * WIDE] = WG[h]

    def store(t):
        return pltpu.make_async_copy(
            C4.at[t, :, pl.ds(0, ROWS), :], out.at[:, :, pl.ds(t * LANES, LANES)], out_sem.at[t]
        )

    for h in range(CHUNKS):
        all_of(h, IR, r2).wait()

        def add(p, carry):
            for k in range(PER):
                lanes = pl.ds(k * LANES, LANES)
                parts = [IR[h, part, rows_of(p), lanes].astype(F32) for part in range(3)]
                for r in range(2):
                    value = jnp.concatenate([parts[r], parts[2][8 * r : 8 * r + 8]], axis=0)
                    rows = pl.ds(2 * p + r, DIRS, stride=RING)
                    C[h * PER + k, rows, :] = C[h * PER + k, rows, :] + value
            return carry

        lax.fori_loop(0, n, add, 0)
        for k in range(PER):
            store(h * PER + k).start()

    for t in range(TILES):
        store(t).wait()

    for h in range(CHUNKS):
        all_of(h, S, s1).wait()
        all_of(h, IS, s2).wait()
    for side, there in ((0, has_prev), (1, has_next)):

        @pl.when(there)
        def _(side=side):
            meta_copies(side).wait_send()
            for h in range(CHUNKS):
                halo_copies(h, side).wait_send()


def shards(n, slabs, forcing, state, wind, cg, turn, sea, sign, w_in, w_out, ww):
    angle = (np.arange(DIRS) + 0.5) * (2.0 * math.pi / DIRS)
    along = jnp.asarray(
        np.stack([0.5 * np.abs(np.cos(angle)), 0.5 * np.abs(np.sin(angle))]).astype(np.float32)
    )
    hbm = pl.BlockSpec(memory_space=pl.ANY)
    vmem = pl.BlockSpec(memory_space=pltpu.VMEM)
    smem = pl.BlockSpec(memory_space=pltpu.SMEM)
    sems = pltpu.SemaphoreType.DMA
    field = (TILES, DIRS, RING, LANES)
    fluxes = (TILES + 2, DIRS * RING, LANES)
    cells = (TILES, RING, LANES)
    message = (CHUNKS, 3, 16 * n, WIDE)
    return pl.pallas_call(
        functools.partial(kernel, n, slabs),
        out_shape=(
            jax.ShapeDtypeStruct(forcing.shape, F32),
            jax.ShapeDtypeStruct(wind.shape, F32),
        ),
        in_specs=[hbm] * 9 + [smem] * 2,
        out_specs=(hbm, vmem),
        scratch_shapes=[
            pltpu.VMEM(field, F32),
            pltpu.VMEM(field, F32),
            pltpu.VMEM(fluxes, F32),
            pltpu.VMEM(fluxes, F32),
            pltpu.VMEM(cells, F32),
            pltpu.VMEM(cells, F32),
            pltpu.VMEM(cells, F32),
            pltpu.VMEM(cells, F32),
            pltpu.VMEM((CHUNKS, 2, 3, 16, WIDE), BF16),
            pltpu.VMEM((CHUNKS, 2, 3, 16, WIDE), BF16),
            pltpu.VMEM((2, 2, TILES * LANES), F32),
            pltpu.VMEM((2, 2, TILES * LANES), F32),
            pltpu.VMEM(message, BF16),
            pltpu.VMEM(message, BF16),
            pltpu.VMEM(message, BF16),
            pltpu.VMEM(message, BF16),
            pltpu.VMEM((ROWS, TILES * LANES), jnp.int32),
            pltpu.VMEM((ROWS, TILES * LANES), jnp.int32),
            pltpu.VMEM((ROWS, TILES * LANES), jnp.int32),
            pltpu.VMEM(wind.shape, F32),
            pltpu.VMEM(ww.shape, F32),
            pltpu.VMEM((CHUNKS, COMPS, 2, WIDE), BF16),
            pltpu.VMEM(w_in.shape, BF16),
            pltpu.VMEM(w_out.shape, BF16),
            pltpu.VMEM((2, COMPS, 2 * COMPS), BF16),
            pltpu.VMEM((2, HID, 512), BF16),
            pltpu.VMEM((COMPS, HID), BF16),
            pltpu.VMEM((2, HID, WIDE), F32),
            pltpu.VMEM((HID, WIDE), BF16),
            pltpu.VMEM((HID, LANES), F32),
            pltpu.VMEM((CHUNKS, 2, WIDE), F32),
            sems((TILES,)),
            sems((7 + CHUNKS,)),
            sems((CHUNKS, 2)),
            sems((CHUNKS, 2)),
            sems((2,)),
            sems((2,)),
            sems((CHUNKS,)),
            sems((CHUNKS,)),
            sems((CHUNKS,)),
            sems((CHUNKS,)),
            sems((TILES,)),
        ],
        compiler_params=pltpu.CompilerParams(
            collective_id=0, has_side_effects=True, vmem_limit_bytes=58 << 20
        ),
        name="adjoint_window",
    )(forcing, state, w_in, w_out, cg, turn, sea, wind, ww, sign, along)


def solution(mesh):
    placed = (
        P("comp", "space", None),
        P(None, ("space", "comp"), None),
        P(("space", "comp"), None),
        P("comp", "space", None),
        P("comp", "space", None),
        P("space", None),
        P(),
        P(),
        P(),
        P(),
    )
    return jax.shard_map(
        functools.partial(shards, mesh.shape["comp"], mesh.shape["space"]),
        mesh=mesh,
        in_specs=placed,
        out_specs=(P("comp", "space", None), P(("space", "comp"), None)),
        check_vma=False,
    )
```

```python
import functools
import math

import jax
import jax.numpy as jnp
import numpy as np
from jax import lax
from jax.experimental import pallas as pl
from jax.experimental.pallas import tpu as pltpu
from jax.sharding import PartitionSpec as P

MESH = pl.DeviceIdType.MESH
DIRS = 24
LANES = 128
ROWS = 32
RING = 40
TILES = 8
CHUNKS = 4
PER = TILES // CHUNKS
WIDE = PER * LANES
HID = 1536
BLOCK = 256
COMPS = 384
F32 = jnp.float32
BF16 = jnp.bfloat16


def iota(shape, dim):
    return lax.broadcasted_iota(jnp.int32, shape, dim)


def picks(mask):
    return jnp.where(mask, 1.0, 0.0).astype(BF16)


def kernel(
    n, slabs,
    forcing, fs, w_in_hbm, w_out_hbm, cg_hbm, turn_hbm, sea_hbm, wind_hbm, ww_hbm, sign, along,
    D4, wgrad,
    C4, Q0, Q1, CM, TM, MK, TN, NO, SO,
    HS, HR, S, R, IS, IR,
    cg, turn, sea, wind, ww, FS4, w_in, w_out, E, WT, A, G, WH, WW, WG,
    load_sem, w_sem, hs_sem, hr_sem, s1, r1, s2, r2,
):
    me = lax.axis_index("comp")
    slab = lax.axis_index("space")
    C = C4.reshape(TILES, DIRS * RING, LANES)
    D = D4.reshape(TILES, DIRS * RING, LANES)

    def load(t):
        return pltpu.make_async_copy(
            forcing.at[:, :, pl.ds(t * LANES, LANES)], C4.at[t, :, pl.ds(0, ROWS), :], load_sem.at[t]
        )

    FS = FS4.reshape(CHUNKS, 2 * COMPS, WIDE)
    maps = [
        pltpu.make_async_copy(cg_hbm.at[0], cg, w_sem.at[2]),
        pltpu.make_async_copy(turn_hbm.at[0], turn, w_sem.at[3]),
        pltpu.make_async_copy(sea_hbm, sea, w_sem.at[4]),
    ]
    for copy in maps:
        copy.start()
    for t in range(TILES):
        load(t).start()
    weights = [
        pltpu.make_async_copy(wind_hbm, wind, w_sem.at[5 + CHUNKS]),
        pltpu.make_async_copy(ww_hbm, ww, w_sem.at[6 + CHUNKS]),
        pltpu.make_async_copy(w_in_hbm, w_in, w_sem.at[0]),
        pltpu.make_async_copy(w_out_hbm, w_out, w_sem.at[1]),
    ] + [
        pltpu.make_async_copy(
            fs.at[:, :, pl.ds(h * WIDE, WIDE)], FS4.at[h], w_sem.at[5 + h]
        )
        for h in range(CHUNKS)
    ]

    barrier = pltpu.get_barrier_semaphore()

    def greet(step, carry):
        pl.semaphore_signal(
            barrier, inc=1, device_id={"comp": lax.rem(me + step, n)}, device_id_type=MESH
        )
        return carry

    lax.fori_loop(1, n, greet, 0)
    has_prev = slab > 0
    has_next = slab < slabs - 1
    sides = ((0, has_prev), (1, has_next))

    @pl.when(has_prev)
    def _():
        pl.semaphore_signal(barrier, inc=1, device_id={"space": slab - 1}, device_id_type=MESH)

    @pl.when(has_next)
    def _():
        pl.semaphore_signal(barrier, inc=1, device_id={"space": slab + 1}, device_id_type=MESH)

    for copy in weights:
        copy.start()

    def halo_copy(h, side):
        peer = slab - 1 if side == 0 else slab + 1
        return pltpu.make_async_remote_copy(
            src_ref=HS.at[h, side], dst_ref=HR.at[h, 1 - side],
            send_sem=hs_sem.at[h, side], recv_sem=hr_sem.at[h, 1 - side],
            device_id={"space": peer}, device_id_type=MESH,
        )

    def halo_arrived(h, side):
        peer = slab - 1 if side == 0 else slab + 1
        return pltpu.make_async_remote_copy(
            src_ref=HS.at[h, side], dst_ref=HR.at[h, side],
            send_sem=hs_sem.at[h, side], recv_sem=hr_sem.at[h, side],
            device_id={"space": peer}, device_id_type=MESH,
        )

    for side, there in sides:

        @pl.when(jnp.logical_not(there))
        def _(side=side):
            HR[:, side] = jnp.zeros((CHUNKS, 3, 16, WIDE), BF16)

    zero = jnp.zeros((DIRS, LANES), F32)
    for t in range(TILES):
        for i in (ROWS, RING - 1):
            Q0[t + 1, pl.ds(i, DIRS, stride=RING), :] = zero
            Q1[t + 1, pl.ds(i, DIRS, stride=RING), :] = zero

    def clear(d, carry):
        rows = pl.ds(pl.multiple_of(d * RING, 8), RING)
        zero = jnp.zeros((RING, LANES), F32)
        for q in (Q0, Q1):
            q[0, rows, :] = zero
            q[TILES + 1, rows, :] = zero
        return carry

    lax.fori_loop(0, DIRS, clear, 0)

    for d in range(DIRS):
        ay = along[1, d]
        north = ay * (0.5 + 0.5 * sign[1, d].astype(F32))
        NO[d : d + 1, :] = jnp.full((1, LANES), north, F32)
        SO[d : d + 1, :] = jnp.full((1, LANES), ay - north, F32)

    for copy in maps:
        copy.wait()
    for t in range(TILES):
        lanes = slice(t * LANES, (t + 1) * LANES)
        level = turn[:, lanes].astype(F32)
        mask = sea[:, lanes].astype(F32)
        MK[t] = mask
        CM[t] = (0.1 + 0.8 * cg[:, lanes].astype(F32) / 7.0) * mask
        TM[t] = (0.3 * jnp.abs(level - 3.5) / 3.5) * mask
        TN[t] = level

    def weigh(t, carry):
        load(t).wait()
        flow = CM[t]

        def one(d, carry):
            rows = pl.ds(pl.multiple_of(d * RING, 8), ROWS)
            Q0[t + 1, rows, :] = flow * C[t, rows, :]
            return carry

        return lax.fori_loop(0, DIRS, one, carry, unroll=4)

    def packed(first, second):
        mixed = jnp.concatenate([first[16:], second[16:]], axis=0)
        return first[:16].astype(BF16), second[:16].astype(BF16), mixed.astype(BF16)

    def unpacked(parts):
        parts = [part.astype(F32) for part in parts]
        return [
            jnp.concatenate([parts[r], parts[2][8 * r : 8 * r + 8]], axis=0) for r in range(2)
        ]

    def send_halo(h):
        for k in range(PER):
            t = h * PER + k
            lanes = pl.ds(k * LANES, LANES)
            for side, row in ((0, 0), (1, ROWS - 1)):
                rows = pl.ds(row, DIRS, stride=RING)
                for part, value in enumerate(packed(Q0[t + 1, rows, :], Q1[t + 1, rows, :])):
                    HS[h, side, part, :, lanes] = value
        for side, there in sides:

            @pl.when(there)
            def _(side=side):
                halo_copy(h, side).start()

    def take_halo(h):
        for side, there in sides:

            @pl.when(there)
            def _(side=side):
                halo_arrived(h, side).wait_recv()

        for k in range(PER):
            t = h * PER + k
            lanes = pl.ds(k * LANES, LANES)
            for side, row, beyond, weight in ((0, 0, RING - 1, SO), (1, ROWS - 1, ROWS, NO)):
                before, after = unpacked([HR[h, side, part, :, lanes] for part in range(3)])
                rows = pl.ds(row, DIRS, stride=RING)
                inflow = weight[...] * before
                D[t, rows, :] = D[t, rows, :] + inflow
                Q1[t + 1, rows, :] = Q1[t + 1, rows, :] + CM[t, row : row + 1, :] * inflow
                Q1[t + 1, pl.ds(beyond, DIRS, stride=RING), :] = after

    lane = iota((ROWS, LANES), 1)

    def step(t, state, q, result, next_q):
        flow = CM[t]
        turns = TM[t]
        mask = MK[t]
        up = TN[t] >= 4.0

        def one(d, carry):
            ring = pl.ds(pl.multiple_of(d * RING, 8), RING)
            rows = pl.ds(pl.multiple_of(d * RING, 8), ROWS)
            above = pl.ds(pl.multiple_of(lax.rem(d + 1, DIRS) * RING, 8), ROWS)
            below = pl.ds(pl.multiple_of(lax.rem(d + DIRS - 1, DIRS) * RING, 8), ROWS)
            ax, ay = along[0, d], along[1, d]
            toward = sign[0, d]
            north = ay * (0.5 + 0.5 * sign[1, d].astype(F32))
            south = ay - north
            c = state[t, rows, :]
            around = q[t + 1, ring, :]
            here = around[:ROWS]
            edge = jnp.where(toward > 0, 0, LANES - 1)
            shift = jnp.where(toward > 0, LANES - 1, 1)
            beside = q[t + 1 + toward, rows, :]
            from_side = pltpu.roll(jnp.where(lane == edge, beside, here), shift, 1)
            from_north = pltpu.roll(around, RING - 1, 0)[:ROWS]
            from_south = pltpu.roll(around, 1, 0)[:ROWS]
            turned = turns * (jnp.where(up, state[t, above, :], state[t, below, :]) - c)
            new = (
                mask * c
                + turned
                + ax * from_side
                + (north * from_north + south * from_south)
                - (ax + ay) * here
            )
            result[t, rows, :] = new
            if next_q is not None:
                next_q[t + 1, rows, :] = flow * new
            return carry

        lax.fori_loop(0, DIRS, one, 0, unroll=True)

    def first_step(t, carry):
        step(t, C, Q0, D, Q1)
        return carry

    def second_step(t, carry):
        step(t, D, Q1, C, None)
        return carry

    def rows_of(p):
        return pl.ds(pl.multiple_of(p * 16, 16), 16)

    def exchange(h, p, source, target, send, recv):
        return pltpu.make_async_remote_copy(
            src_ref=source.at[h, :, rows_of(p), :], dst_ref=target.at[h, :, rows_of(me), :],
            send_sem=send.at[h], recv_sem=recv.at[h],
            device_id={"comp": p}, device_id_type=MESH,
        )

    def all_of(h, buffer, sem):
        others = buffer.at[h, :, pl.ds(0, 16 * (n - 1)), :]
        return pltpu.make_async_copy(others, others, sem.at[h])

    def dispatch(h, inner, outer):
        def one(i, carry):
            p = lax.rem(me + i, n)
            within = jnp.logical_and(p > 0, p < n - 1)

            def go():
                for k in range(PER):
                    t = h * PER + k
                    lanes = pl.ds(k * LANES, LANES)
                    first = C[t, pl.ds(2 * p, DIRS, stride=RING), :]
                    second = C[t, pl.ds(2 * p + 1, DIRS, stride=RING), :]
                    for part, value in enumerate(packed(first, second)):
                        S[h, part, rows_of(p), lanes] = value

                @pl.when(i > 0)
                def _():
                    exchange(h, p, S, R, s1, r1).start()

            if inner and outer:
                go()
            else:
                pl.when(within if inner else jnp.logical_not(within))(go)
            return carry

        lax.fori_loop(0, n, one, 0)
        if outer:
            R[h, :, rows_of(me), :] = S[h, :, rows_of(me), :]

    lax.fori_loop(0, 2 * PER + 1, weigh, 0)
    lax.fori_loop(0, 2 * PER, first_step, 0)
    pl.semaphore_wait(barrier, n - 1 + has_prev.astype(jnp.int32) + has_next.astype(jnp.int32))
    send_halo(0)
    send_halo(1)
    lax.fori_loop(0, PER, second_step, 0)
    dispatch(0, True, False)
    lax.fori_loop(2 * PER + 1, TILES, weigh, 0)

    def rest(h, carry):
        lax.fori_loop(h * PER, h * PER + PER, first_step, 0)
        send_halo(h)
        return carry

    lax.fori_loop(2, CHUNKS, rest, 0)
    take_halo(0)
    take_halo(1)
    lax.fori_loop(0, PER, second_step, 0)
    dispatch(0, False, True)

    def propagate(h, carry):
        @pl.when(h < CHUNKS - 1)
        def _():
            take_halo(h + 1)

        lax.fori_loop(h * PER, h * PER + PER, second_step, 0)
        dispatch(h, True, True)
        return carry

    lax.fori_loop(1, CHUNKS, propagate, 0)
    for copy in weights:
        copy.wait()
    wide = (COMPS, 2 * COMPS)
    for r in range(2):
        E[r] = picks(iota(wide, 1) == 2 * iota(wide, 0) + r)

    square = (COMPS, COMPS)
    place = iota(square, 0)
    rest = place - 256
    comp = jnp.where(
        place < 256,
        24 * lax.shift_right_logical(place, 4) + (place & 15),
        24 * lax.shift_right_arithmetic(rest, 3) + 16 + (rest & 7),
    )
    order = picks(iota(square, 1) == comp)
    nt = (((1,), (1,)), ((), ()))
    for m in range(HID // BLOCK):
        A[:, m * BLOCK : (m + 1) * BLOCK] = lax.dot_general(
            order, w_in[m * BLOCK : (m + 1) * BLOCK, :], nt, preferred_element_type=F32
        ).astype(BF16)

    tall = (COMPS, 512)
    place = iota(tall, 1)
    within = place & 15
    base = 24 * lax.shift_right_logical(place & 255, 4)
    eye = picks(iota((BLOCK, BLOCK), 0) == iota((BLOCK, BLOCK), 1))
    chosen = []
    for r in range(2):
        mixed = jnp.where(
            lax.shift_right_logical(within, 3) == r, base + 16 + (within & 7), -1
        )
        chosen.append(picks(iota(tall, 0) == jnp.where(place < 256, base + within, mixed)))
    for m in range(HID // BLOCK):
        rows = slice(m * BLOCK, (m + 1) * BLOCK)
        turned = lax.dot_general(eye, w_out[:, rows], nt, preferred_element_type=F32).astype(BF16)
        for r in range(2):
            WT[r, rows, :] = jnp.dot(turned, chosen[r], preferred_element_type=F32).astype(BF16)

    for b in range(HID // LANES):
        row = ww[b * LANES : (b + 1) * LANES].reshape(1, LANES)
        WW[b * LANES : (b + 1) * LANES, :] = jnp.broadcast_to(row, (LANES, LANES)).T

    def block_rows(m):
        return pl.ds(pl.multiple_of(m * BLOCK, BLOCK), BLOCK)

    def slopes(h):
        for r in range(2):
            cells = jnp.dot(E[r], FS[h], preferred_element_type=F32).astype(BF16)
            gusts = wind[r : r + 1, pl.ds(pl.multiple_of(h * WIDE, WIDE), WIDE)]

            def block(m, carry):
                rows = block_rows(m)
                winds = jnp.concatenate([WW[rows, :]] * PER, axis=1)
                squash = jnp.tanh(
                    jnp.dot(w_in[rows, :], cells, preferred_element_type=F32) + winds * gusts
                )
                G[r, rows, :] = 1.0 - squash * squash
                return carry

            lax.fori_loop(0, HID // BLOCK, block, 0, unroll=True)

    def network(h, carry):
        slopes(h)
        all_of(h, R, r1).wait()
        tails = []
        for r in range(2):
            cells = jnp.concatenate([R[h, r], R[h, 2]], axis=0)

            def block(m, total):
                rows = block_rows(m)
                pulled = jnp.dot(WT[r, rows, :], cells, preferred_element_type=F32)
                weighted = G[r, rows, :] * pulled
                WH[rows, :] = weighted.astype(BF16)
                winds = jnp.concatenate([WW[rows, :]] * PER, axis=1)
                return total + jnp.sum((winds * weighted).reshape(BLOCK // 8, 8, WIDE), axis=0)

            total = lax.fori_loop(
                0, HID // BLOCK, block, jnp.zeros((8, WIDE), F32), unroll=True
            )
            WG[h, r : r + 1, :] = jnp.sum(total, axis=0, keepdims=True)
            increment = jnp.dot(A[...], WH[...], preferred_element_type=F32)
            IS[h, r] = increment[:256].astype(BF16)
            tails.append(increment[256:].reshape(16, 1, 8, WIDE))
        IS[h, 2] = jnp.concatenate(tails, axis=1).reshape(256, WIDE).astype(BF16)

        def send(i, carry):
            exchange(h, lax.rem(me + i, n), IS, IR, s2, r2).start()
            return carry

        lax.fori_loop(1, n, send, 0)
        IR[h, :, rows_of(me), :] = IS[h, :, rows_of(me), :]
        return carry

    lax.fori_loop(0, CHUNKS, network, 0)

    for h in range(CHUNKS):
        wgrad[:, h * WIDE : (h + 1) * WIDE] = WG[h]

    def collect(h, carry):
        all_of(h, IR, r2).wait()

        def add(p, carry):
            for k in range(PER):
                t = h * PER + k
                lanes = pl.ds(k * LANES, LANES)
                values = unpacked([IR[h, part, rows_of(p), lanes] for part in range(3)])
                for r in range(2):
                    rows = pl.ds(2 * p + r, DIRS, stride=RING)
                    D[t, rows, :] = C[t, rows, :] + values[r]
            return carry

        return lax.fori_loop(0, n, add, carry, unroll=2)

    lax.fori_loop(0, CHUNKS, collect, 0)
    for h in range(CHUNKS):
        all_of(h, S, s1).wait()
        all_of(h, IS, s2).wait()
    for side, there in sides:

        @pl.when(there)
        def _(side=side):
            for h in range(CHUNKS):
                halo_copy(h, side).wait_send()


def finish(total, slope, out, wgrad, out_sem, w_sem):
    def store(t):
        return pltpu.make_async_copy(
            total.at[t, :, pl.ds(0, ROWS), :], out.at[:, :, pl.ds(t * LANES, LANES)], out_sem.at[t]
        )

    copies = [store(t) for t in range(TILES)] + [pltpu.make_async_copy(slope, wgrad, w_sem)]
    for copy in copies:
        copy.start()
    for copy in copies:
        copy.wait()


def shards(n, slabs, forcing, state, wind, cg, turn, sea, sign, w_in, w_out, ww):
    angle = (np.arange(DIRS) + 0.5) * (2.0 * math.pi / DIRS)
    along = jnp.asarray(
        np.stack([0.5 * np.abs(np.cos(angle)), 0.5 * np.abs(np.sin(angle))]).astype(np.float32)
    )
    hbm = pl.BlockSpec(memory_space=pl.ANY)
    vmem = pl.BlockSpec(memory_space=pltpu.VMEM)
    smem = pl.BlockSpec(memory_space=pltpu.SMEM)
    sems = pltpu.SemaphoreType.DMA
    field = (TILES, DIRS, RING, LANES)
    fluxes = (TILES + 2, DIRS * RING, LANES)
    cells = (TILES, ROWS, LANES)
    message = (CHUNKS, 3, 16 * n, WIDE)
    total, slope = pl.pallas_call(
        functools.partial(kernel, n, slabs),
        out_shape=(
            pltpu.VMEM(field, F32),
            pltpu.VMEM(wind.shape, F32),
        ),
        in_specs=[hbm] * 9 + [smem] * 2,
        out_specs=(vmem, vmem),
        scratch_shapes=[
            pltpu.VMEM(field, F32),
            pltpu.VMEM(fluxes, F32),
            pltpu.VMEM(fluxes, F32),
            pltpu.VMEM(cells, F32),
            pltpu.VMEM(cells, F32),
            pltpu.VMEM(cells, F32),
            pltpu.VMEM(cells, F32),
            pltpu.VMEM((DIRS, LANES), F32),
            pltpu.VMEM((DIRS, LANES), F32),
            pltpu.VMEM((CHUNKS, 2, 3, 16, WIDE), BF16),
            pltpu.VMEM((CHUNKS, 2, 3, 16, WIDE), BF16),
            pltpu.VMEM(message, BF16),
            pltpu.VMEM(message, BF16),
            pltpu.VMEM(message, BF16),
            pltpu.VMEM(message, BF16),
            pltpu.VMEM((ROWS, TILES * LANES), jnp.int32),
            pltpu.VMEM((ROWS, TILES * LANES), jnp.int32),
            pltpu.VMEM((ROWS, TILES * LANES), jnp.int32),
            pltpu.VMEM(wind.shape, F32),
            pltpu.VMEM(ww.shape, F32),
            pltpu.VMEM((CHUNKS, COMPS, 2, WIDE), BF16),
            pltpu.VMEM(w_in.shape, BF16),
            pltpu.VMEM(w_out.shape, BF16),
            pltpu.VMEM((2, COMPS, 2 * COMPS), BF16),
            pltpu.VMEM((2, HID, 512), BF16),
            pltpu.VMEM((COMPS, HID), BF16),
            pltpu.VMEM((2, HID, WIDE), F32),
            pltpu.VMEM((HID, WIDE), BF16),
            pltpu.VMEM((HID, LANES), F32),
            pltpu.VMEM((CHUNKS, 2, WIDE), F32),
            sems((TILES,)),
            sems((7 + CHUNKS,)),
            sems((CHUNKS, 2)),
            sems((CHUNKS, 2)),
            sems((CHUNKS,)),
            sems((CHUNKS,)),
            sems((CHUNKS,)),
            sems((CHUNKS,)),
        ],
        compiler_params=pltpu.CompilerParams(
            collective_id=0, has_side_effects=True, vmem_limit_bytes=58 << 20
        ),
        name="adjoint_window",
    )(forcing, state, w_in, w_out, cg, turn, sea, wind, ww, sign, along)
    return pl.pallas_call(
        finish,
        out_shape=(
            jax.ShapeDtypeStruct(forcing.shape, F32),
            jax.ShapeDtypeStruct(wind.shape, F32),
        ),
        in_specs=[vmem] * 2,
        out_specs=(hbm, hbm),
        scratch_shapes=[sems((TILES,)), sems],
        compiler_params=pltpu.CompilerParams(vmem_limit_bytes=16 << 20),
        name="finish",
    )(total, slope)


def solution(mesh):
    placed = (
        P("comp", "space", None),
        P(None, ("space", "comp"), None),
        P(("space", "comp"), None),
        P("comp", "space", None),
        P("comp", "space", None),
        P("space", None),
        P(),
        P(),
        P(),
        P(),
    )
    return jax.shard_map(
        functools.partial(shards, mesh.shape["comp"], mesh.shape["space"]),
        mesh=mesh,
        in_specs=placed,
        out_specs=(P("comp", "space", None), P(("space", "comp"), None)),
        check_vma=False,
    )
```

```python
import functools
import math

import jax
import jax.numpy as jnp
import numpy as np
from jax import lax
from jax.experimental import pallas as pl
from jax.experimental.pallas import tpu as pltpu
from jax.sharding import PartitionSpec as P

MESH = pl.DeviceIdType.MESH
DIRS = 24
LANES = 128
ROWS = 32
RING = 40
TILES = 8
CHUNKS = 4
PER = TILES // CHUNKS
EARLY = 2
WIDE = PER * LANES
HID = 1536
BLOCK = 256
COMPS = 384
F32 = jnp.float32
BF16 = jnp.bfloat16


def iota(shape, dim):
    return lax.broadcasted_iota(jnp.int32, shape, dim)


def picks(mask):
    return jnp.where(mask, 1.0, 0.0).astype(BF16)


def kernel(
    n, slabs,
    forcing, fs, w_in_hbm, w_out_hbm, cg_hbm, turn_hbm, sea_hbm, wind_hbm, ww_hbm, sign, along,
    D4, wgrad,
    C4, Q0, Q1, CM, TM, MK, TN, NO, SO,
    HS, HR, S, R, IS, IR,
    cg, turn, sea, wind, ww, FS4, w_in, w_out, E, WT, A, G, WH, WW, WG,
    load_sem, w_sem, hs_sem, hr_sem, s1, r1, s2, r2,
):
    me = lax.axis_index("comp")
    slab = lax.axis_index("space")

    barrier = pltpu.get_barrier_semaphore()
    has_prev = slab > 0
    has_next = slab < slabs - 1
    sides = ((0, has_prev), (1, has_next))

    @pl.when(has_prev)
    def _():
        pl.semaphore_signal(barrier, inc=1, device_id={"space": slab - 1}, device_id_type=MESH)

    @pl.when(has_next)
    def _():
        pl.semaphore_signal(barrier, inc=1, device_id={"space": slab + 1}, device_id_type=MESH)

    C = C4.reshape(TILES, DIRS * RING, LANES)
    D = D4.reshape(TILES, DIRS * RING, LANES)

    def load(t):
        return pltpu.make_async_copy(
            forcing.at[:, :, pl.ds(t * LANES, LANES)], C4.at[t, :, pl.ds(0, ROWS), :], load_sem.at[t]
        )

    FS = FS4.reshape(CHUNKS, 2 * COMPS, WIDE)
    maps = [
        pltpu.make_async_copy(cg_hbm.at[0], cg, w_sem.at[2]),
        pltpu.make_async_copy(turn_hbm.at[0], turn, w_sem.at[3]),
        pltpu.make_async_copy(sea_hbm, sea, w_sem.at[4]),
    ]
    for copy in maps:
        copy.start()
    for t in range(TILES):
        load(t).start()
    weights = [
        pltpu.make_async_copy(wind_hbm, wind, w_sem.at[5 + CHUNKS]),
        pltpu.make_async_copy(ww_hbm, ww, w_sem.at[6 + CHUNKS]),
        pltpu.make_async_copy(w_in_hbm, w_in, w_sem.at[0]),
        pltpu.make_async_copy(w_out_hbm, w_out, w_sem.at[1]),
    ] + [
        pltpu.make_async_copy(
            fs.at[:, :, pl.ds(h * WIDE, WIDE)], FS4.at[h], w_sem.at[5 + h]
        )
        for h in range(CHUNKS)
    ]

    def greet(step, carry):
        pl.semaphore_signal(
            barrier, inc=1, device_id={"comp": lax.rem(me + step, n)}, device_id_type=MESH
        )
        return carry

    lax.fori_loop(1, n, greet, 0)

    for copy in weights:
        copy.start()

    def halo_copy(h, side):
        peer = slab - 1 if side == 0 else slab + 1
        return pltpu.make_async_remote_copy(
            src_ref=HS.at[h, side], dst_ref=HR.at[h, 1 - side],
            send_sem=hs_sem.at[h, side], recv_sem=hr_sem.at[h, 1 - side],
            device_id={"space": peer}, device_id_type=MESH,
        )

    def halo_arrived(h, side):
        peer = slab - 1 if side == 0 else slab + 1
        return pltpu.make_async_remote_copy(
            src_ref=HS.at[h, side], dst_ref=HR.at[h, side],
            send_sem=hs_sem.at[h, side], recv_sem=hr_sem.at[h, side],
            device_id={"space": peer}, device_id_type=MESH,
        )

    for side, there in sides:

        @pl.when(jnp.logical_not(there))
        def _(side=side):
            HR[:, side] = jnp.zeros((CHUNKS, 3, 16, WIDE), BF16)

    zero = jnp.zeros((DIRS, LANES), F32)
    for t in range(TILES):
        for i in (ROWS, RING - 1):
            Q0[t + 1, pl.ds(i, DIRS, stride=RING), :] = zero
            Q1[t + 1, pl.ds(i, DIRS, stride=RING), :] = zero

    def clear(d, carry):
        rows = pl.ds(pl.multiple_of(d * RING, 8), RING)
        zero = jnp.zeros((RING, LANES), F32)
        for q in (Q0, Q1):
            q[0, rows, :] = zero
            q[TILES + 1, rows, :] = zero
        return carry

    lax.fori_loop(0, DIRS, clear, 0)

    for d in range(DIRS):
        ay = along[1, d]
        north = ay * (0.5 + 0.5 * sign[1, d].astype(F32))
        NO[d : d + 1, :] = jnp.full((1, LANES), north, F32)
        SO[d : d + 1, :] = jnp.full((1, LANES), ay - north, F32)

    for copy in maps:
        copy.wait()
    for t in range(TILES):
        lanes = slice(t * LANES, (t + 1) * LANES)
        level = turn[:, lanes].astype(F32)
        mask = sea[:, lanes].astype(F32)
        MK[t] = mask
        CM[t] = (0.1 + 0.8 * cg[:, lanes].astype(F32) / 7.0) * mask
        TM[t] = (0.3 * jnp.abs(level - 3.5) / 3.5) * mask
        TN[t] = level

    def weigh(t, carry):
        load(t).wait()
        flow = CM[t]

        def one(d, carry):
            rows = pl.ds(pl.multiple_of(d * RING, 8), ROWS)
            Q0[t + 1, rows, :] = flow * C[t, rows, :]
            return carry

        return lax.fori_loop(0, DIRS, one, carry, unroll=4)

    def packed(first, second):
        mixed = jnp.concatenate([first[16:], second[16:]], axis=0)
        return first[:16].astype(BF16), second[:16].astype(BF16), mixed.astype(BF16)

    def unpacked(parts):
        parts = [part.astype(F32) for part in parts]
        return [
            jnp.concatenate([parts[r], parts[2][8 * r : 8 * r + 8]], axis=0) for r in range(2)
        ]

    def pack_halo(h):
        for k in range(PER):
            t = h * PER + k
            lanes = pl.ds(k * LANES, LANES)
            for side, row in ((0, 0), (1, ROWS - 1)):
                rows = pl.ds(row, DIRS, stride=RING)
                for part, value in enumerate(packed(Q0[t + 1, rows, :], Q1[t + 1, rows, :])):
                    HS[h, side, part, :, lanes] = value

    def send_halo(h):
        for side, there in sides:

            @pl.when(there)
            def _(side=side):
                halo_copy(h, side).start()

    def take_halo(h):
        for side, there in sides:

            @pl.when(there)
            def _(side=side):
                halo_arrived(h, side).wait_recv()

        for k in range(PER):
            t = h * PER + k
            lanes = pl.ds(k * LANES, LANES)
            for side, row, beyond, weight in ((0, 0, RING - 1, SO), (1, ROWS - 1, ROWS, NO)):
                before, after = unpacked([HR[h, side, part, :, lanes] for part in range(3)])
                rows = pl.ds(row, DIRS, stride=RING)
                inflow = weight[...] * before
                D[t, rows, :] = D[t, rows, :] + inflow
                Q1[t + 1, rows, :] = Q1[t + 1, rows, :] + CM[t, row : row + 1, :] * inflow
                Q1[t + 1, pl.ds(beyond, DIRS, stride=RING), :] = after

    lane = iota((ROWS, LANES), 1)

    def step(t, state, q, result, next_q):
        flow = CM[t]
        turns = TM[t]
        mask = MK[t]
        up = TN[t] >= 4.0

        def one(d, carry):
            ring = pl.ds(pl.multiple_of(d * RING, 8), RING)
            rows = pl.ds(pl.multiple_of(d * RING, 8), ROWS)
            above = pl.ds(pl.multiple_of(lax.rem(d + 1, DIRS) * RING, 8), ROWS)
            below = pl.ds(pl.multiple_of(lax.rem(d + DIRS - 1, DIRS) * RING, 8), ROWS)
            ax, ay = along[0, d], along[1, d]
            toward = sign[0, d]
            north = ay * (0.5 + 0.5 * sign[1, d].astype(F32))
            south = ay - north
            c = state[t, rows, :]
            around = q[t + 1, ring, :]
            here = around[:ROWS]
            edge = jnp.where(toward > 0, 0, LANES - 1)
            shift = jnp.where(toward > 0, LANES - 1, 1)
            beside = q[t + 1 + toward, rows, :]
            from_side = pltpu.roll(jnp.where(lane == edge, beside, here), shift, 1)
            from_north = pltpu.roll(around, RING - 1, 0)[:ROWS]
            from_south = pltpu.roll(around, 1, 0)[:ROWS]
            turned = turns * (jnp.where(up, state[t, above, :], state[t, below, :]) - c)
            new = (
                mask * c
                + turned
                + ax * from_side
                + (north * from_north + south * from_south)
                - (ax + ay) * here
            )
            result[t, rows, :] = new
            if next_q is not None:
                next_q[t + 1, rows, :] = flow * new
            return carry

        lax.fori_loop(0, DIRS, one, 0, unroll=True)

    def first_step(t, carry):
        step(t, C, Q0, D, Q1)
        return carry

    def second_step(t, carry):
        step(t, D, Q1, C, None)
        return carry

    def rows_of(p):
        return pl.ds(pl.multiple_of(p * 16, 16), 16)

    def exchange(h, p, source, target, send, recv):
        return pltpu.make_async_remote_copy(
            src_ref=source.at[h, :, rows_of(p), :], dst_ref=target.at[h, :, rows_of(me), :],
            send_sem=send.at[h], recv_sem=recv.at[h],
            device_id={"comp": p}, device_id_type=MESH,
        )

    def all_of(h, buffer, sem):
        others = buffer.at[h, :, pl.ds(0, 16 * (n - 1)), :]
        return pltpu.make_async_copy(others, others, sem.at[h])

    def dispatch(h, inner, outer):
        def one(i, carry):
            p = lax.rem(me + i, n)
            within = jnp.logical_and(p > 0, p < n - 1)

            def go():
                for k in range(PER):
                    t = h * PER + k
                    lanes = pl.ds(k * LANES, LANES)
                    first = C[t, pl.ds(2 * p, DIRS, stride=RING), :]
                    second = C[t, pl.ds(2 * p + 1, DIRS, stride=RING), :]
                    for part, value in enumerate(packed(first, second)):
                        S[h, part, rows_of(p), lanes] = value

                @pl.when(i > 0)
                def _():
                    exchange(h, p, S, R, s1, r1).start()

            if inner and outer:
                go()
            else:
                pl.when(within if inner else jnp.logical_not(within))(go)
            return carry

        lax.fori_loop(0, n, one, 0)
        if outer:
            R[h, :, rows_of(me), :] = S[h, :, rows_of(me), :]

    lax.fori_loop(0, TILES, weigh, 0)
    lax.fori_loop(0, TILES, first_step, 0)

    def pack_all(h, carry):
        pack_halo(h)
        return carry

    lax.fori_loop(0, CHUNKS, pack_all, 0)
    pl.semaphore_wait(barrier, n - 1 + has_prev.astype(jnp.int32) + has_next.astype(jnp.int32))
    for h in range(CHUNKS):
        send_halo(h)

    def ahead(h, carry):
        lax.fori_loop(h * PER, h * PER + PER, second_step, 0)
        dispatch(h, True, False)
        return carry

    lax.fori_loop(0, EARLY, ahead, 0)

    def behind(h, carry):
        take_halo(h)

        @pl.when(h > 0)
        def _():
            lax.fori_loop((h - 1) * PER, h * PER, second_step, 0)

            @pl.when(h <= EARLY)
            def _():
                dispatch(h - 1, False, True)

            @pl.when(h > EARLY)
            def _():
                dispatch(h - 1, True, True)

        return carry

    lax.fori_loop(0, CHUNKS, behind, 0)
    lax.fori_loop(TILES - PER, TILES, second_step, 0)
    dispatch(CHUNKS - 1, True, True)

    for copy in weights:
        copy.wait()
    wide = (COMPS, 2 * COMPS)
    for r in range(2):
        E[r] = picks(iota(wide, 1) == 2 * iota(wide, 0) + r)

    square = (COMPS, COMPS)
    place = iota(square, 0)
    rest = place - 256
    comp = jnp.where(
        place < 256,
        24 * lax.shift_right_logical(place, 4) + (place & 15),
        24 * lax.shift_right_arithmetic(rest, 3) + 16 + (rest & 7),
    )
    order = picks(iota(square, 1) == comp)
    nt = (((1,), (1,)), ((), ()))
    for m in range(HID // BLOCK):
        A[:, m * BLOCK : (m + 1) * BLOCK] = lax.dot_general(
            order, w_in[m * BLOCK : (m + 1) * BLOCK, :], nt, preferred_element_type=F32
        ).astype(BF16)

    tall = (COMPS, 512)
    place = iota(tall, 1)
    within = place & 15
    base = 24 * lax.shift_right_logical(place & 255, 4)
    eye = picks(iota((BLOCK, BLOCK), 0) == iota((BLOCK, BLOCK), 1))
    chosen = []
    for r in range(2):
        mixed = jnp.where(
            lax.shift_right_logical(within, 3) == r, base + 16 + (within & 7), -1
        )
        chosen.append(picks(iota(tall, 0) == jnp.where(place < 256, base + within, mixed)))
    for m in range(HID // BLOCK):
        rows = slice(m * BLOCK, (m + 1) * BLOCK)
        turned = lax.dot_general(eye, w_out[:, rows], nt, preferred_element_type=F32).astype(BF16)
        for r in range(2):
            WT[r, rows, :] = jnp.dot(turned, chosen[r], preferred_element_type=F32).astype(BF16)

    for b in range(HID // LANES):
        row = ww[b * LANES : (b + 1) * LANES].reshape(1, LANES)
        WW[b * LANES : (b + 1) * LANES, :] = jnp.broadcast_to(row, (LANES, LANES)).T

    def block_rows(m):
        return pl.ds(pl.multiple_of(m * BLOCK, BLOCK), BLOCK)

    def slopes(h):
        for r in range(2):
            cells = jnp.dot(E[r], FS[h], preferred_element_type=F32).astype(BF16)
            gusts = wind[r : r + 1, pl.ds(pl.multiple_of(h * WIDE, WIDE), WIDE)]

            def block(m, carry):
                rows = block_rows(m)
                winds = jnp.concatenate([WW[rows, :]] * PER, axis=1)
                squash = jnp.tanh(
                    jnp.dot(w_in[rows, :], cells, preferred_element_type=F32) + winds * gusts
                )
                G[r, rows, :] = 1.0 - squash * squash
                return carry

            lax.fori_loop(0, HID // BLOCK, block, 0, unroll=True)

    def network(h, carry):
        slopes(h)
        all_of(h, R, r1).wait()
        tails = []
        for r in range(2):
            cells = jnp.concatenate([R[h, r], R[h, 2]], axis=0)

            def block(m, total):
                rows = block_rows(m)
                pulled = jnp.dot(WT[r, rows, :], cells, preferred_element_type=F32)
                weighted = G[r, rows, :] * pulled
                WH[rows, :] = weighted.astype(BF16)
                winds = jnp.concatenate([WW[rows, :]] * PER, axis=1)
                return total + jnp.sum((winds * weighted).reshape(BLOCK // 8, 8, WIDE), axis=0)

            total = lax.fori_loop(
                0, HID // BLOCK, block, jnp.zeros((8, WIDE), F32), unroll=True
            )
            WG[h, r : r + 1, :] = jnp.sum(total, axis=0, keepdims=True)
            increment = jnp.dot(A[...], WH[...], preferred_element_type=F32)
            IS[h, r] = increment[:256].astype(BF16)
            tails.append(increment[256:].reshape(16, 1, 8, WIDE))
        IS[h, 2] = jnp.concatenate(tails, axis=1).reshape(256, WIDE).astype(BF16)

        def send(i, carry):
            exchange(h, lax.rem(me + i, n), IS, IR, s2, r2).start()
            return carry

        lax.fori_loop(1, n, send, 0)
        IR[h, :, rows_of(me), :] = IS[h, :, rows_of(me), :]
        return carry

    lax.fori_loop(0, CHUNKS, network, 0)

    for h in range(CHUNKS):
        wgrad[:, h * WIDE : (h + 1) * WIDE] = WG[h]

    def collect(h, carry):
        all_of(h, IR, r2).wait()

        def add(p, carry):
            for k in range(PER):
                t = h * PER + k
                lanes = pl.ds(k * LANES, LANES)
                values = unpacked([IR[h, part, rows_of(p), lanes] for part in range(3)])
                for r in range(2):
                    rows = pl.ds(2 * p + r, DIRS, stride=RING)
                    D[t, rows, :] = C[t, rows, :] + values[r]
            return carry

        return lax.fori_loop(0, n, add, carry, unroll=4)

    lax.fori_loop(0, CHUNKS, collect, 0)
    for h in range(CHUNKS):
        all_of(h, S, s1).wait()
        all_of(h, IS, s2).wait()
    for side, there in sides:

        @pl.when(there)
        def _(side=side):
            for h in range(CHUNKS):
                halo_copy(h, side).wait_send()


def finish(total, slope, out, wgrad, out_sem, w_sem):
    def store(t):
        return pltpu.make_async_copy(
            total.at[t, :, pl.ds(0, ROWS), :], out.at[:, :, pl.ds(t * LANES, LANES)], out_sem.at[t]
        )

    copies = [store(t) for t in range(TILES)] + [pltpu.make_async_copy(slope, wgrad, w_sem)]
    for copy in copies:
        copy.start()
    for copy in copies:
        copy.wait()


def shards(n, slabs, forcing, state, wind, cg, turn, sea, sign, w_in, w_out, ww):
    angle = (np.arange(DIRS) + 0.5) * (2.0 * math.pi / DIRS)
    along = jnp.asarray(
        np.stack([0.5 * np.abs(np.cos(angle)), 0.5 * np.abs(np.sin(angle))]).astype(np.float32)
    )
    hbm = pl.BlockSpec(memory_space=pl.ANY)
    vmem = pl.BlockSpec(memory_space=pltpu.VMEM)
    smem = pl.BlockSpec(memory_space=pltpu.SMEM)
    sems = pltpu.SemaphoreType.DMA
    field = (TILES, DIRS, RING, LANES)
    fluxes = (TILES + 2, DIRS * RING, LANES)
    cells = (TILES, ROWS, LANES)
    message = (CHUNKS, 3, 16 * n, WIDE)
    total, slope = pl.pallas_call(
        functools.partial(kernel, n, slabs),
        out_shape=(
            pltpu.VMEM(field, F32),
            pltpu.VMEM(wind.shape, F32),
        ),
        in_specs=[hbm] * 9 + [smem] * 2,
        out_specs=(vmem, vmem),
        scratch_shapes=[
            pltpu.VMEM(field, F32),
            pltpu.VMEM(fluxes, F32),
            pltpu.VMEM(fluxes, F32),
            pltpu.VMEM(cells, F32),
            pltpu.VMEM(cells, F32),
            pltpu.VMEM(cells, F32),
            pltpu.VMEM(cells, F32),
            pltpu.VMEM((DIRS, LANES), F32),
            pltpu.VMEM((DIRS, LANES), F32),
            pltpu.VMEM((CHUNKS, 2, 3, 16, WIDE), BF16),
            pltpu.VMEM((CHUNKS, 2, 3, 16, WIDE), BF16),
            pltpu.VMEM(message, BF16),
            pltpu.VMEM(message, BF16),
            pltpu.VMEM(message, BF16),
            pltpu.VMEM(message, BF16),
            pltpu.VMEM((ROWS, TILES * LANES), jnp.int32),
            pltpu.VMEM((ROWS, TILES * LANES), jnp.int32),
            pltpu.VMEM((ROWS, TILES * LANES), jnp.int32),
            pltpu.VMEM(wind.shape, F32),
            pltpu.VMEM(ww.shape, F32),
            pltpu.VMEM((CHUNKS, COMPS, 2, WIDE), BF16),
            pltpu.VMEM(w_in.shape, BF16),
            pltpu.VMEM(w_out.shape, BF16),
            pltpu.VMEM((2, COMPS, 2 * COMPS), BF16),
            pltpu.VMEM((2, HID, 512), BF16),
            pltpu.VMEM((COMPS, HID), BF16),
            pltpu.VMEM((2, HID, WIDE), F32),
            pltpu.VMEM((HID, WIDE), BF16),
            pltpu.VMEM((HID, LANES), F32),
            pltpu.VMEM((CHUNKS, 2, WIDE), F32),
            sems((TILES,)),
            sems((7 + CHUNKS,)),
            sems((CHUNKS, 2)),
            sems((CHUNKS, 2)),
            sems((CHUNKS,)),
            sems((CHUNKS,)),
            sems((CHUNKS,)),
            sems((CHUNKS,)),
        ],
        compiler_params=pltpu.CompilerParams(
            collective_id=0, has_side_effects=True, vmem_limit_bytes=58 << 20
        ),
        name="adjoint_window",
    )(forcing, state, w_in, w_out, cg, turn, sea, wind, ww, sign, along)
    return pl.pallas_call(
        finish,
        out_shape=(
            jax.ShapeDtypeStruct(forcing.shape, F32),
            jax.ShapeDtypeStruct(wind.shape, F32),
        ),
        in_specs=[vmem] * 2,
        out_specs=(hbm, hbm),
        scratch_shapes=[sems((TILES,)), sems],
        compiler_params=pltpu.CompilerParams(vmem_limit_bytes=16 << 20),
        name="finish",
    )(total, slope)


def solution(mesh):
    placed = (
        P("comp", "space", None),
        P(None, ("space", "comp"), None),
        P(("space", "comp"), None),
        P("comp", "space", None),
        P("comp", "space", None),
        P("space", None),
        P(),
        P(),
        P(),
        P(),
    )
    return jax.shard_map(
        functools.partial(shards, mesh.shape["comp"], mesh.shape["space"]),
        mesh=mesh,
        in_specs=placed,
        out_specs=(P("comp", "space", None), P(("space", "comp"), None)),
        check_vma=False,
    )
```

```python
import functools
import math

import jax
import jax.numpy as jnp
import numpy as np
from jax import lax
from jax.experimental import pallas as pl
from jax.experimental.pallas import tpu as pltpu
from jax.sharding import PartitionSpec as P

MESH = pl.DeviceIdType.MESH
DIRS = 24
LANES = 128
ROWS = 32
RING = 40
TILES = 8
CHUNKS = 4
PER = TILES // CHUNKS
EARLY = 3
WIDE = PER * LANES
HID = 1536
BLOCK = 256
COMPS = 384
F32 = jnp.float32
BF16 = jnp.bfloat16


def iota(shape, dim):
    return lax.broadcasted_iota(jnp.int32, shape, dim)


def picks(mask):
    return jnp.where(mask, 1.0, 0.0).astype(BF16)


def kernel(
    n, slabs,
    forcing, fs, w_in_hbm, w_out_hbm, cg_hbm, turn_hbm, sea_hbm, wind_hbm, ww_hbm, sign, along,
    D4, wgrad,
    C4, Q0, Q1, CM, TM, MK, TN, NO, SO,
    HS, HR, S, R, IS, IR,
    cg, turn, sea, wind, ww, FS4, w_in, w_out, E, WT, A, G, WH, WW, WG,
    load_sem, w_sem, hs_sem, hr_sem, s1, r1, s2, r2,
):
    me = lax.axis_index("comp")
    slab = lax.axis_index("space")

    barrier = pltpu.get_barrier_semaphore()
    has_prev = slab > 0
    has_next = slab < slabs - 1
    sides = ((0, has_prev), (1, has_next))

    @pl.when(has_prev)
    def _():
        pl.semaphore_signal(barrier, inc=1, device_id={"space": slab - 1}, device_id_type=MESH)

    @pl.when(has_next)
    def _():
        pl.semaphore_signal(barrier, inc=1, device_id={"space": slab + 1}, device_id_type=MESH)

    C = C4.reshape(TILES, DIRS * RING, LANES)
    D = D4.reshape(TILES, DIRS * RING, LANES)

    def load(t):
        return pltpu.make_async_copy(
            forcing.at[:, :, pl.ds(t * LANES, LANES)], C4.at[t, :, pl.ds(0, ROWS), :], load_sem.at[t]
        )

    FS = FS4.reshape(CHUNKS, 2 * COMPS, WIDE)
    maps = [
        pltpu.make_async_copy(cg_hbm.at[0], cg, w_sem.at[2]),
        pltpu.make_async_copy(turn_hbm.at[0], turn, w_sem.at[3]),
        pltpu.make_async_copy(sea_hbm, sea, w_sem.at[4]),
    ]
    for copy in maps:
        copy.start()
    for t in range(TILES):
        load(t).start()
    weights = [
        pltpu.make_async_copy(wind_hbm, wind, w_sem.at[5 + CHUNKS]),
        pltpu.make_async_copy(ww_hbm, ww, w_sem.at[6 + CHUNKS]),
        pltpu.make_async_copy(w_in_hbm, w_in, w_sem.at[0]),
        pltpu.make_async_copy(w_out_hbm, w_out, w_sem.at[1]),
    ] + [
        pltpu.make_async_copy(
            fs.at[:, :, pl.ds(h * WIDE, WIDE)], FS4.at[h], w_sem.at[5 + h]
        )
        for h in range(CHUNKS)
    ]

    def greet(step, carry):
        pl.semaphore_signal(
            barrier, inc=1, device_id={"comp": lax.rem(me + step, n)}, device_id_type=MESH
        )
        return carry

    lax.fori_loop(1, n, greet, 0)

    for copy in weights:
        copy.start()

    def halo_copy(h, side):
        peer = slab - 1 if side == 0 else slab + 1
        return pltpu.make_async_remote_copy(
            src_ref=HS.at[h, side], dst_ref=HR.at[h, 1 - side],
            send_sem=hs_sem.at[h, side], recv_sem=hr_sem.at[h, 1 - side],
            device_id={"space": peer}, device_id_type=MESH,
        )

    def halo_arrived(h, side):
        peer = slab - 1 if side == 0 else slab + 1
        return pltpu.make_async_remote_copy(
            src_ref=HS.at[h, side], dst_ref=HR.at[h, side],
            send_sem=hs_sem.at[h, side], recv_sem=hr_sem.at[h, side],
            device_id={"space": peer}, device_id_type=MESH,
        )

    for side, there in sides:

        @pl.when(jnp.logical_not(there))
        def _(side=side):
            HR[:, side] = jnp.zeros((CHUNKS, 3, 16, WIDE), BF16)

    zero = jnp.zeros((DIRS, LANES), F32)
    for t in range(TILES):
        for i in (ROWS, RING - 1):
            Q0[t + 1, pl.ds(i, DIRS, stride=RING), :] = zero
            Q1[t + 1, pl.ds(i, DIRS, stride=RING), :] = zero

    def clear(d, carry):
        rows = pl.ds(pl.multiple_of(d * RING, 8), RING)
        zero = jnp.zeros((RING, LANES), F32)
        for q in (Q0, Q1):
            q[0, rows, :] = zero
            q[TILES + 1, rows, :] = zero
        return carry

    lax.fori_loop(0, DIRS, clear, 0)

    for d in range(DIRS):
        ay = along[1, d]
        north = ay * (0.5 + 0.5 * sign[1, d].astype(F32))
        NO[d : d + 1, :] = jnp.full((1, LANES), north, F32)
        SO[d : d + 1, :] = jnp.full((1, LANES), ay - north, F32)

    for copy in maps:
        copy.wait()
    for t in range(TILES):
        lanes = slice(t * LANES, (t + 1) * LANES)
        level = turn[:, lanes].astype(F32)
        mask = sea[:, lanes].astype(F32)
        MK[t] = mask
        CM[t] = (0.1 + 0.8 * cg[:, lanes].astype(F32) / 7.0) * mask
        TM[t] = (0.3 * jnp.abs(level - 3.5) / 3.5) * mask
        TN[t] = level

    def weigh(t, carry):
        load(t).wait()
        flow = CM[t]

        def one(d, carry):
            rows = pl.ds(pl.multiple_of(d * RING, 8), ROWS)
            Q0[t + 1, rows, :] = flow * C[t, rows, :]
            return carry

        return lax.fori_loop(0, DIRS, one, carry, unroll=4)

    def packed(first, second):
        mixed = jnp.concatenate([first[16:], second[16:]], axis=0)
        return first[:16].astype(BF16), second[:16].astype(BF16), mixed.astype(BF16)

    def unpacked(parts):
        parts = [part.astype(F32) for part in parts]
        return [
            jnp.concatenate([parts[r], parts[2][8 * r : 8 * r + 8]], axis=0) for r in range(2)
        ]

    def pack_halo(h):
        for k in range(PER):
            t = h * PER + k
            lanes = pl.ds(k * LANES, LANES)
            for side, row in ((0, 0), (1, ROWS - 1)):
                rows = pl.ds(row, DIRS, stride=RING)
                for part, value in enumerate(packed(Q0[t + 1, rows, :], Q1[t + 1, rows, :])):
                    HS[h, side, part, :, lanes] = value

    def send_halo(h):
        for side, there in sides:

            @pl.when(there)
            def _(side=side):
                halo_copy(h, side).start()

    def take_halo(h):
        for side, there in sides:

            @pl.when(there)
            def _(side=side):
                halo_arrived(h, side).wait_recv()

        for k in range(PER):
            t = h * PER + k
            lanes = pl.ds(k * LANES, LANES)
            for side, row, beyond, weight in ((0, 0, RING - 1, SO), (1, ROWS - 1, ROWS, NO)):
                before, after = unpacked([HR[h, side, part, :, lanes] for part in range(3)])
                rows = pl.ds(row, DIRS, stride=RING)
                inflow = weight[...] * before
                D[t, rows, :] = D[t, rows, :] + inflow
                Q1[t + 1, rows, :] = Q1[t + 1, rows, :] + CM[t, row : row + 1, :] * inflow
                Q1[t + 1, pl.ds(beyond, DIRS, stride=RING), :] = after

    lane = iota((ROWS, LANES), 1)

    def step(t, state, q, result, next_q):
        flow = CM[t]
        turns = TM[t]
        mask = MK[t]
        up = TN[t] >= 4.0

        def one(d, carry):
            ring = pl.ds(pl.multiple_of(d * RING, 8), RING)
            rows = pl.ds(pl.multiple_of(d * RING, 8), ROWS)
            above = pl.ds(pl.multiple_of(lax.rem(d + 1, DIRS) * RING, 8), ROWS)
            below = pl.ds(pl.multiple_of(lax.rem(d + DIRS - 1, DIRS) * RING, 8), ROWS)
            ax, ay = along[0, d], along[1, d]
            toward = sign[0, d]
            north = ay * (0.5 + 0.5 * sign[1, d].astype(F32))
            south = ay - north
            c = state[t, rows, :]
            around = q[t + 1, ring, :]
            here = around[:ROWS]
            edge = jnp.where(toward > 0, 0, LANES - 1)
            shift = jnp.where(toward > 0, LANES - 1, 1)
            beside = q[t + 1 + toward, rows, :]
            from_side = pltpu.roll(jnp.where(lane == edge, beside, here), shift, 1)
            from_north = pltpu.roll(around, RING - 1, 0)[:ROWS]
            from_south = pltpu.roll(around, 1, 0)[:ROWS]
            turned = turns * (jnp.where(up, state[t, above, :], state[t, below, :]) - c)
            new = (
                mask * c
                + turned
                + ax * from_side
                + (north * from_north + south * from_south)
                - (ax + ay) * here
            )
            result[t, rows, :] = new
            if next_q is not None:
                next_q[t + 1, rows, :] = flow * new
            return carry

        lax.fori_loop(0, DIRS, one, 0, unroll=True)

    def first_step(t, carry):
        step(t, C, Q0, D, Q1)
        return carry

    def second_step(t, carry):
        step(t, D, Q1, C, None)
        return carry

    def rows_of(p):
        return pl.ds(pl.multiple_of(p * 16, 16), 16)

    def exchange(h, p, source, target, send, recv):
        return pltpu.make_async_remote_copy(
            src_ref=source.at[h, :, rows_of(p), :], dst_ref=target.at[h, :, rows_of(me), :],
            send_sem=send.at[h], recv_sem=recv.at[h],
            device_id={"comp": p}, device_id_type=MESH,
        )

    def all_of(h, buffer, sem):
        others = buffer.at[h, :, pl.ds(0, 16 * (n - 1)), :]
        return pltpu.make_async_copy(others, others, sem.at[h])

    def dispatch(h, inner, outer):
        def one(i, carry):
            p = lax.rem(me + i, n)
            within = jnp.logical_and(p > 0, p < n - 1)

            def go():
                for k in range(PER):
                    t = h * PER + k
                    lanes = pl.ds(k * LANES, LANES)
                    first = C[t, pl.ds(2 * p, DIRS, stride=RING), :]
                    second = C[t, pl.ds(2 * p + 1, DIRS, stride=RING), :]
                    for part, value in enumerate(packed(first, second)):
                        S[h, part, rows_of(p), lanes] = value

                @pl.when(i > 0)
                def _():
                    exchange(h, p, S, R, s1, r1).start()

            if inner and outer:
                go()
            else:
                pl.when(within if inner else jnp.logical_not(within))(go)
            return carry

        lax.fori_loop(0, n, one, 0)
        if outer:
            R[h, :, rows_of(me), :] = S[h, :, rows_of(me), :]

    lax.fori_loop(0, TILES, weigh, 0)
    lax.fori_loop(0, TILES, first_step, 0)

    def pack_all(h, carry):
        pack_halo(h)
        return carry

    lax.fori_loop(0, CHUNKS, pack_all, 0)
    pl.semaphore_wait(barrier, n - 1 + has_prev.astype(jnp.int32) + has_next.astype(jnp.int32))
    for h in range(CHUNKS):
        send_halo(h)

    def ahead(h, carry):
        lax.fori_loop(h * PER, h * PER + PER, second_step, 0)
        dispatch(h, True, False)
        return carry

    lax.fori_loop(0, EARLY, ahead, 0)

    def behind(h, carry):
        take_halo(h)

        @pl.when(h > 0)
        def _():
            lax.fori_loop((h - 1) * PER, h * PER, second_step, 0)

            @pl.when(h <= EARLY)
            def _():
                dispatch(h - 1, False, True)

            @pl.when(h > EARLY)
            def _():
                dispatch(h - 1, True, True)

        return carry

    lax.fori_loop(0, CHUNKS, behind, 0)
    lax.fori_loop(TILES - PER, TILES, second_step, 0)
    dispatch(CHUNKS - 1, True, True)

    for copy in weights:
        copy.wait()
    wide = (COMPS, 2 * COMPS)
    for r in range(2):
        E[r] = picks(iota(wide, 1) == 2 * iota(wide, 0) + r)

    square = (COMPS, COMPS)
    place = iota(square, 0)
    rest = place - 256
    comp = jnp.where(
        place < 256,
        24 * lax.shift_right_logical(place, 4) + (place & 15),
        24 * lax.shift_right_arithmetic(rest, 3) + 16 + (rest & 7),
    )
    order = picks(iota(square, 1) == comp)
    nt = (((1,), (1,)), ((), ()))
    for m in range(HID // BLOCK):
        A[:, m * BLOCK : (m + 1) * BLOCK] = lax.dot_general(
            order, w_in[m * BLOCK : (m + 1) * BLOCK, :], nt, preferred_element_type=F32
        ).astype(BF16)

    tall = (COMPS, 512)
    place = iota(tall, 1)
    within = place & 15
    base = 24 * lax.shift_right_logical(place & 255, 4)
    eye = picks(iota((BLOCK, BLOCK), 0) == iota((BLOCK, BLOCK), 1))
    chosen = []
    for r in range(2):
        mixed = jnp.where(
            lax.shift_right_logical(within, 3) == r, base + 16 + (within & 7), -1
        )
        chosen.append(picks(iota(tall, 0) == jnp.where(place < 256, base + within, mixed)))
    for m in range(HID // BLOCK):
        rows = slice(m * BLOCK, (m + 1) * BLOCK)
        turned = lax.dot_general(eye, w_out[:, rows], nt, preferred_element_type=F32).astype(BF16)
        for r in range(2):
            WT[r, rows, :] = jnp.dot(turned, chosen[r], preferred_element_type=F32).astype(BF16)

    for b in range(HID // LANES):
        row = ww[b * LANES : (b + 1) * LANES].reshape(1, LANES)
        WW[b * LANES : (b + 1) * LANES, :] = jnp.broadcast_to(row, (LANES, LANES)).T

    def block_rows(m):
        return pl.ds(pl.multiple_of(m * BLOCK, BLOCK), BLOCK)

    def slopes(h):
        for r in range(2):
            cells = jnp.dot(E[r], FS[h], preferred_element_type=F32).astype(BF16)
            gusts = wind[r : r + 1, pl.ds(pl.multiple_of(h * WIDE, WIDE), WIDE)]

            def block(m, carry):
                rows = block_rows(m)
                winds = jnp.concatenate([WW[rows, :]] * PER, axis=1)
                squash = jnp.tanh(
                    jnp.dot(w_in[rows, :], cells, preferred_element_type=F32) + winds * gusts
                )
                G[r, rows, :] = 1.0 - squash * squash
                return carry

            lax.fori_loop(0, HID // BLOCK, block, 0, unroll=True)

    def network(h, carry):
        slopes(h)
        all_of(h, R, r1).wait()
        tails = []
        for r in range(2):
            cells = jnp.concatenate([R[h, r], R[h, 2]], axis=0)

            def block(m, total):
                rows = block_rows(m)
                pulled = jnp.dot(WT[r, rows, :], cells, preferred_element_type=F32)
                weighted = G[r, rows, :] * pulled
                WH[rows, :] = weighted.astype(BF16)
                winds = jnp.concatenate([WW[rows, :]] * PER, axis=1)
                return total + jnp.sum((winds * weighted).reshape(BLOCK // 8, 8, WIDE), axis=0)

            total = lax.fori_loop(
                0, HID // BLOCK, block, jnp.zeros((8, WIDE), F32), unroll=True
            )
            WG[h, r : r + 1, :] = jnp.sum(total, axis=0, keepdims=True)
            increment = jnp.dot(A[...], WH[...], preferred_element_type=F32)
            IS[h, r] = increment[:256].astype(BF16)
            tails.append(increment[256:].reshape(16, 1, 8, WIDE))
        IS[h, 2] = jnp.concatenate(tails, axis=1).reshape(256, WIDE).astype(BF16)

        def send(i, carry):
            exchange(h, lax.rem(me + i, n), IS, IR, s2, r2).start()
            return carry

        lax.fori_loop(1, n, send, 0)
        IR[h, :, rows_of(me), :] = IS[h, :, rows_of(me), :]
        return carry

    lax.fori_loop(0, CHUNKS, network, 0)

    for h in range(CHUNKS):
        wgrad[:, h * WIDE : (h + 1) * WIDE] = WG[h]

    def collect(h, carry):
        all_of(h, IR, r2).wait()

        def add(p, carry):
            for k in range(PER):
                t = h * PER + k
                lanes = pl.ds(k * LANES, LANES)
                values = unpacked([IR[h, part, rows_of(p), lanes] for part in range(3)])
                for r in range(2):
                    rows = pl.ds(2 * p + r, DIRS, stride=RING)
                    D[t, rows, :] = C[t, rows, :] + values[r]
            return carry

        return lax.fori_loop(0, n, add, carry, unroll=4)

    lax.fori_loop(0, CHUNKS, collect, 0)
    for h in range(CHUNKS):
        all_of(h, S, s1).wait()
        all_of(h, IS, s2).wait()
    for side, there in sides:

        @pl.when(there)
        def _(side=side):
            for h in range(CHUNKS):
                halo_copy(h, side).wait_send()


def finish(total, slope, out, wgrad, out_sem, w_sem):
    def store(t):
        return pltpu.make_async_copy(
            total.at[t, :, pl.ds(0, ROWS), :], out.at[:, :, pl.ds(t * LANES, LANES)], out_sem.at[t]
        )

    copies = [store(t) for t in range(TILES)] + [pltpu.make_async_copy(slope, wgrad, w_sem)]
    for copy in copies:
        copy.start()
    for copy in copies:
        copy.wait()


def shards(n, slabs, forcing, state, wind, cg, turn, sea, sign, w_in, w_out, ww):
    angle = (np.arange(DIRS) + 0.5) * (2.0 * math.pi / DIRS)
    along = jnp.asarray(
        np.stack([0.5 * np.abs(np.cos(angle)), 0.5 * np.abs(np.sin(angle))]).astype(np.float32)
    )
    hbm = pl.BlockSpec(memory_space=pl.ANY)
    vmem = pl.BlockSpec(memory_space=pltpu.VMEM)
    smem = pl.BlockSpec(memory_space=pltpu.SMEM)
    sems = pltpu.SemaphoreType.DMA
    field = (TILES, DIRS, RING, LANES)
    fluxes = (TILES + 2, DIRS * RING, LANES)
    cells = (TILES, ROWS, LANES)
    message = (CHUNKS, 3, 16 * n, WIDE)
    total, slope = pl.pallas_call(
        functools.partial(kernel, n, slabs),
        out_shape=(
            pltpu.VMEM(field, F32),
            pltpu.VMEM(wind.shape, F32),
        ),
        in_specs=[hbm] * 9 + [smem] * 2,
        out_specs=(vmem, vmem),
        scratch_shapes=[
            pltpu.VMEM(field, F32),
            pltpu.VMEM(fluxes, F32),
            pltpu.VMEM(fluxes, F32),
            pltpu.VMEM(cells, F32),
            pltpu.VMEM(cells, F32),
            pltpu.VMEM(cells, F32),
            pltpu.VMEM(cells, F32),
            pltpu.VMEM((DIRS, LANES), F32),
            pltpu.VMEM((DIRS, LANES), F32),
            pltpu.VMEM((CHUNKS, 2, 3, 16, WIDE), BF16),
            pltpu.VMEM((CHUNKS, 2, 3, 16, WIDE), BF16),
            pltpu.VMEM(message, BF16),
            pltpu.VMEM(message, BF16),
            pltpu.VMEM(message, BF16),
            pltpu.VMEM(message, BF16),
            pltpu.VMEM((ROWS, TILES * LANES), jnp.int32),
            pltpu.VMEM((ROWS, TILES * LANES), jnp.int32),
            pltpu.VMEM((ROWS, TILES * LANES), jnp.int32),
            pltpu.VMEM(wind.shape, F32),
            pltpu.VMEM(ww.shape, F32),
            pltpu.VMEM((CHUNKS, COMPS, 2, WIDE), BF16),
            pltpu.VMEM(w_in.shape, BF16),
            pltpu.VMEM(w_out.shape, BF16),
            pltpu.VMEM((2, COMPS, 2 * COMPS), BF16),
            pltpu.VMEM((2, HID, 512), BF16),
            pltpu.VMEM((COMPS, HID), BF16),
            pltpu.VMEM((2, HID, WIDE), F32),
            pltpu.VMEM((HID, WIDE), BF16),
            pltpu.VMEM((HID, LANES), F32),
            pltpu.VMEM((CHUNKS, 2, WIDE), F32),
            sems((TILES,)),
            sems((7 + CHUNKS,)),
            sems((CHUNKS, 2)),
            sems((CHUNKS, 2)),
            sems((CHUNKS,)),
            sems((CHUNKS,)),
            sems((CHUNKS,)),
            sems((CHUNKS,)),
        ],
        compiler_params=pltpu.CompilerParams(
            collective_id=0, has_side_effects=True, vmem_limit_bytes=58 << 20
        ),
        name="adjoint_window",
    )(forcing, state, w_in, w_out, cg, turn, sea, wind, ww, sign, along)
    return pl.pallas_call(
        finish,
        out_shape=(
            jax.ShapeDtypeStruct(forcing.shape, F32),
            jax.ShapeDtypeStruct(wind.shape, F32),
        ),
        in_specs=[vmem] * 2,
        out_specs=(hbm, hbm),
        scratch_shapes=[sems((TILES,)), sems],
        compiler_params=pltpu.CompilerParams(vmem_limit_bytes=16 << 20),
        name="finish",
    )(total, slope)


def solution(mesh):
    placed = (
        P("comp", "space", None),
        P(None, ("space", "comp"), None),
        P(("space", "comp"), None),
        P("comp", "space", None),
        P("comp", "space", None),
        P("space", None),
        P(),
        P(),
        P(),
        P(),
    )
    return jax.shard_map(
        functools.partial(shards, mesh.shape["comp"], mesh.shape["space"]),
        mesh=mesh,
        in_specs=placed,
        out_specs=(P("comp", "space", None), P(("space", "comp"), None)),
        check_vma=False,
    )
```

```python
import functools
import math

import jax
import jax.numpy as jnp
import numpy as np
from jax import lax
from jax.experimental import pallas as pl
from jax.experimental.pallas import tpu as pltpu
from jax.sharding import PartitionSpec as P

MESH = pl.DeviceIdType.MESH
DIRS = 24
LANES = 128
ROWS = 32
RING = 40
TILES = 8
CHUNKS = 4
PER = TILES // CHUNKS
EARLY = 3
WIDE = PER * LANES
HID = 1536
BLOCK = 256
COMPS = 384
F32 = jnp.float32
BF16 = jnp.bfloat16


def iota(shape, dim):
    return lax.broadcasted_iota(jnp.int32, shape, dim)


def picks(mask):
    return jnp.where(mask, 1.0, 0.0).astype(BF16)


def kernel(
    n, slabs,
    forcing, fs, w_in_hbm, w_out_hbm, cg_hbm, turn_hbm, sea_hbm, wind_hbm, ww_hbm, sign, along,
    D4, wgrad,
    C4, Q0, Q1, CM, TM, MK, TN, NO, SO,
    HS, HR, S, R, IS, IR,
    cg, turn, sea, wind, ww, FS4, w_in, w_out, E, WT, A, G, WH, WW, WG,
    load_sem, w_sem, hs_sem, hr_sem, s1, r1, s2, r2,
):
    me = lax.axis_index("comp")
    slab = lax.axis_index("space")

    barrier = pltpu.get_barrier_semaphore()
    has_prev = slab > 0
    has_next = slab < slabs - 1
    sides = ((0, has_prev), (1, has_next))

    @pl.when(has_prev)
    def _():
        pl.semaphore_signal(barrier, inc=1, device_id={"space": slab - 1}, device_id_type=MESH)

    @pl.when(has_next)
    def _():
        pl.semaphore_signal(barrier, inc=1, device_id={"space": slab + 1}, device_id_type=MESH)

    def greet(step, carry):
        pl.semaphore_signal(
            barrier, inc=1, device_id={"comp": lax.rem(me + step, n)}, device_id_type=MESH
        )
        return carry

    lax.fori_loop(1, n, greet, 0)

    C = C4.reshape(TILES, DIRS * RING, LANES)
    D = D4.reshape(TILES, DIRS * RING, LANES)

    def load(t):
        return pltpu.make_async_copy(
            forcing.at[:, :, pl.ds(t * LANES, LANES)], C4.at[t, :, pl.ds(0, ROWS), :], load_sem.at[t]
        )

    FS = FS4.reshape(CHUNKS, 2 * COMPS, WIDE)
    maps = [
        pltpu.make_async_copy(cg_hbm.at[0], cg, w_sem.at[2]),
        pltpu.make_async_copy(turn_hbm.at[0], turn, w_sem.at[3]),
        pltpu.make_async_copy(sea_hbm, sea, w_sem.at[4]),
    ]
    for copy in maps:
        copy.start()
    for t in range(TILES):
        load(t).start()
    weights = [
        pltpu.make_async_copy(wind_hbm, wind, w_sem.at[5 + CHUNKS]),
        pltpu.make_async_copy(ww_hbm, ww, w_sem.at[6 + CHUNKS]),
        pltpu.make_async_copy(w_in_hbm, w_in, w_sem.at[0]),
        pltpu.make_async_copy(w_out_hbm, w_out, w_sem.at[1]),
    ] + [
        pltpu.make_async_copy(
            fs.at[:, :, pl.ds(h * WIDE, WIDE)], FS4.at[h], w_sem.at[5 + h]
        )
        for h in range(CHUNKS)
    ]

    for copy in weights:
        copy.start()

    def halo_copy(h, side):
        peer = slab - 1 if side == 0 else slab + 1
        return pltpu.make_async_remote_copy(
            src_ref=HS.at[h, side], dst_ref=HR.at[h, 1 - side],
            send_sem=hs_sem.at[h, side], recv_sem=hr_sem.at[h, 1 - side],
            device_id={"space": peer}, device_id_type=MESH,
        )

    def halo_arrived(h, side):
        peer = slab - 1 if side == 0 else slab + 1
        return pltpu.make_async_remote_copy(
            src_ref=HS.at[h, side], dst_ref=HR.at[h, side],
            send_sem=hs_sem.at[h, side], recv_sem=hr_sem.at[h, side],
            device_id={"space": peer}, device_id_type=MESH,
        )

    for side, there in sides:

        @pl.when(jnp.logical_not(there))
        def _(side=side):
            HR[:, side] = jnp.zeros((CHUNKS, 3, 16, WIDE), BF16)

    zero = jnp.zeros((DIRS, LANES), F32)
    for t in range(TILES):
        for i in (ROWS, RING - 1):
            Q0[t + 1, pl.ds(i, DIRS, stride=RING), :] = zero
            Q1[t + 1, pl.ds(i, DIRS, stride=RING), :] = zero

    def clear(d, carry):
        rows = pl.ds(pl.multiple_of(d * RING, 8), RING)
        zero = jnp.zeros((RING, LANES), F32)
        for q in (Q0, Q1):
            q[0, rows, :] = zero
            q[TILES + 1, rows, :] = zero
        return carry

    lax.fori_loop(0, DIRS, clear, 0)

    for d in range(DIRS):
        ay = along[1, d]
        north = ay * (0.5 + 0.5 * sign[1, d].astype(F32))
        NO[d : d + 1, :] = jnp.full((1, LANES), north, F32)
        SO[d : d + 1, :] = jnp.full((1, LANES), ay - north, F32)

    for copy in maps:
        copy.wait()
    for t in range(TILES):
        lanes = slice(t * LANES, (t + 1) * LANES)
        level = turn[:, lanes].astype(F32)
        mask = sea[:, lanes].astype(F32)
        MK[t] = mask
        CM[t] = (0.1 + 0.8 * cg[:, lanes].astype(F32) / 7.0) * mask
        TM[t] = (0.3 * jnp.abs(level - 3.5) / 3.5) * mask
        TN[t] = level

    def weigh(t, carry):
        load(t).wait()
        flow = CM[t]

        def one(d, carry):
            rows = pl.ds(pl.multiple_of(d * RING, 8), ROWS)
            Q0[t + 1, rows, :] = flow * C[t, rows, :]
            return carry

        return lax.fori_loop(0, DIRS, one, carry, unroll=4)

    def packed(first, second):
        mixed = jnp.concatenate([first[16:], second[16:]], axis=0)
        return first[:16].astype(BF16), second[:16].astype(BF16), mixed.astype(BF16)

    def unpacked(parts):
        parts = [part.astype(F32) for part in parts]
        return [
            jnp.concatenate([parts[r], parts[2][8 * r : 8 * r + 8]], axis=0) for r in range(2)
        ]

    def pack_halo(h):
        for k in range(PER):
            t = h * PER + k
            lanes = pl.ds(k * LANES, LANES)
            for side, row in ((0, 0), (1, ROWS - 1)):
                rows = pl.ds(row, DIRS, stride=RING)
                for part, value in enumerate(packed(Q0[t + 1, rows, :], Q1[t + 1, rows, :])):
                    HS[h, side, part, :, lanes] = value

    def send_halo(h):
        for side, there in sides:

            @pl.when(there)
            def _(side=side):
                halo_copy(h, side).start()

    def take_halo(h):
        for side, there in sides:

            @pl.when(there)
            def _(side=side):
                halo_arrived(h, side).wait_recv()

        for k in range(PER):
            t = h * PER + k
            lanes = pl.ds(k * LANES, LANES)
            for side, row, beyond, weight in ((0, 0, RING - 1, SO), (1, ROWS - 1, ROWS, NO)):
                before, after = unpacked([HR[h, side, part, :, lanes] for part in range(3)])
                rows = pl.ds(row, DIRS, stride=RING)
                inflow = weight[...] * before
                D[t, rows, :] = D[t, rows, :] + inflow
                Q1[t + 1, rows, :] = Q1[t + 1, rows, :] + CM[t, row : row + 1, :] * inflow
                Q1[t + 1, pl.ds(beyond, DIRS, stride=RING), :] = after

    lane = iota((ROWS, LANES), 1)

    def step(t, state, q, result, next_q):
        flow = CM[t]
        turns = TM[t]
        mask = MK[t]
        up = TN[t] >= 4.0

        def one(d, carry):
            ring = pl.ds(pl.multiple_of(d * RING, 8), RING)
            rows = pl.ds(pl.multiple_of(d * RING, 8), ROWS)
            above = pl.ds(pl.multiple_of(lax.rem(d + 1, DIRS) * RING, 8), ROWS)
            below = pl.ds(pl.multiple_of(lax.rem(d + DIRS - 1, DIRS) * RING, 8), ROWS)
            ax, ay = along[0, d], along[1, d]
            toward = sign[0, d]
            north = ay * (0.5 + 0.5 * sign[1, d].astype(F32))
            south = ay - north
            c = state[t, rows, :]
            around = q[t + 1, ring, :]
            here = around[:ROWS]
            edge = jnp.where(toward > 0, 0, LANES - 1)
            shift = jnp.where(toward > 0, LANES - 1, 1)
            beside = q[t + 1 + toward, rows, :]
            from_side = pltpu.roll(jnp.where(lane == edge, beside, here), shift, 1)
            from_north = pltpu.roll(around, RING - 1, 0)[:ROWS]
            from_south = pltpu.roll(around, 1, 0)[:ROWS]
            turned = turns * (jnp.where(up, state[t, above, :], state[t, below, :]) - c)
            new = (
                mask * c
                + turned
                + ax * from_side
                + (north * from_north + south * from_south)
                - (ax + ay) * here
            )
            result[t, rows, :] = new
            if next_q is not None:
                next_q[t + 1, rows, :] = flow * new
            return carry

        lax.fori_loop(0, DIRS, one, 0, unroll=True)

    def first_step(t, carry):
        step(t, C, Q0, D, Q1)
        return carry

    def second_step(t, carry):
        step(t, D, Q1, C, None)
        return carry

    def rows_of(p):
        return pl.ds(pl.multiple_of(p * 16, 16), 16)

    def exchange(h, p, source, target, send, recv):
        return pltpu.make_async_remote_copy(
            src_ref=source.at[h, :, rows_of(p), :], dst_ref=target.at[h, :, rows_of(me), :],
            send_sem=send.at[h], recv_sem=recv.at[h],
            device_id={"comp": p}, device_id_type=MESH,
        )

    def all_of(h, buffer, sem):
        others = buffer.at[h, :, pl.ds(0, 16 * (n - 1)), :]
        return pltpu.make_async_copy(others, others, sem.at[h])

    def dispatch(h, inner, outer):
        def one(i, carry):
            p = lax.rem(me + i, n)
            within = jnp.logical_and(p > 0, p < n - 1)

            def go():
                for k in range(PER):
                    t = h * PER + k
                    lanes = pl.ds(k * LANES, LANES)
                    first = C[t, pl.ds(2 * p, DIRS, stride=RING), :]
                    second = C[t, pl.ds(2 * p + 1, DIRS, stride=RING), :]
                    for part, value in enumerate(packed(first, second)):
                        S[h, part, rows_of(p), lanes] = value

                @pl.when(i > 0)
                def _():
                    exchange(h, p, S, R, s1, r1).start()

            if inner and outer:
                go()
            else:
                pl.when(within if inner else jnp.logical_not(within))(go)
            return carry

        lax.fori_loop(0, n, one, 0)
        if outer:
            R[h, :, rows_of(me), :] = S[h, :, rows_of(me), :]

    lax.fori_loop(0, TILES, weigh, 0)
    lax.fori_loop(0, TILES, first_step, 0)

    def pack_all(h, carry):
        pack_halo(h)
        return carry

    lax.fori_loop(0, CHUNKS, pack_all, 0)
    pl.semaphore_wait(barrier, n - 1 + has_prev.astype(jnp.int32) + has_next.astype(jnp.int32))
    for h in range(CHUNKS):
        send_halo(h)

    def ahead(h, carry):
        lax.fori_loop(h * PER, h * PER + PER, second_step, 0)
        dispatch(h, True, False)
        return carry

    lax.fori_loop(0, EARLY, ahead, 0)

    def behind(h, carry):
        take_halo(h)

        @pl.when(h > 0)
        def _():
            lax.fori_loop((h - 1) * PER, h * PER, second_step, 0)

            @pl.when(h <= EARLY)
            def _():
                dispatch(h - 1, False, True)

            @pl.when(h > EARLY)
            def _():
                dispatch(h - 1, True, True)

        return carry

    lax.fori_loop(0, CHUNKS, behind, 0)
    lax.fori_loop(TILES - PER, TILES, second_step, 0)
    dispatch(CHUNKS - 1, True, True)

    for copy in weights:
        copy.wait()
    wide = (COMPS, 2 * COMPS)
    for r in range(2):
        E[r] = picks(iota(wide, 1) == 2 * iota(wide, 0) + r)

    square = (COMPS, COMPS)
    place = iota(square, 0)
    rest = place - 256
    comp = jnp.where(
        place < 256,
        24 * lax.shift_right_logical(place, 4) + (place & 15),
        24 * lax.shift_right_arithmetic(rest, 3) + 16 + (rest & 7),
    )
    order = picks(iota(square, 1) == comp)
    nt = (((1,), (1,)), ((), ()))
    for m in range(HID // BLOCK):
        A[:, m * BLOCK : (m + 1) * BLOCK] = lax.dot_general(
            order, w_in[m * BLOCK : (m + 1) * BLOCK, :], nt, preferred_element_type=F32
        ).astype(BF16)

    tall = (COMPS, 512)
    place = iota(tall, 1)
    within = place & 15
    base = 24 * lax.shift_right_logical(place & 255, 4)
    eye = picks(iota((BLOCK, BLOCK), 0) == iota((BLOCK, BLOCK), 1))
    chosen = []
    for r in range(2):
        mixed = jnp.where(
            lax.shift_right_logical(within, 3) == r, base + 16 + (within & 7), -1
        )
        chosen.append(picks(iota(tall, 0) == jnp.where(place < 256, base + within, mixed)))
    for m in range(HID // BLOCK):
        rows = slice(m * BLOCK, (m + 1) * BLOCK)
        turned = lax.dot_general(eye, w_out[:, rows], nt, preferred_element_type=F32).astype(BF16)
        for r in range(2):
            WT[r, rows, :] = jnp.dot(turned, chosen[r], preferred_element_type=F32).astype(BF16)

    for b in range(HID // LANES):
        row = ww[b * LANES : (b + 1) * LANES].reshape(1, LANES)
        WW[b * LANES : (b + 1) * LANES, :] = jnp.broadcast_to(row, (LANES, LANES)).T

    def block_rows(m):
        return pl.ds(pl.multiple_of(m * BLOCK, BLOCK), BLOCK)

    def slopes(h):
        for r in range(2):
            cells = jnp.dot(E[r], FS[h], preferred_element_type=F32).astype(BF16)
            gusts = wind[r : r + 1, pl.ds(pl.multiple_of(h * WIDE, WIDE), WIDE)]

            def block(m, carry):
                rows = block_rows(m)
                winds = jnp.concatenate([WW[rows, :]] * PER, axis=1)
                squash = jnp.tanh(
                    jnp.dot(w_in[rows, :], cells, preferred_element_type=F32) + winds * gusts
                )
                G[r, rows, :] = 1.0 - squash * squash
                return carry

            lax.fori_loop(0, HID // BLOCK, block, 0, unroll=True)

    def network(h, carry):
        slopes(h)
        all_of(h, R, r1).wait()
        tails = []
        for r in range(2):
            cells = jnp.concatenate([R[h, r], R[h, 2]], axis=0)

            def block(m, total):
                rows = block_rows(m)
                pulled = jnp.dot(WT[r, rows, :], cells, preferred_element_type=F32)
                weighted = G[r, rows, :] * pulled
                WH[rows, :] = weighted.astype(BF16)
                winds = jnp.concatenate([WW[rows, :]] * PER, axis=1)
                return total + jnp.sum((winds * weighted).reshape(BLOCK // 8, 8, WIDE), axis=0)

            total = lax.fori_loop(
                0, HID // BLOCK, block, jnp.zeros((8, WIDE), F32), unroll=True
            )
            WG[h, r : r + 1, :] = jnp.sum(total, axis=0, keepdims=True)
            increment = jnp.dot(A[...], WH[...], preferred_element_type=F32)
            IS[h, r] = increment[:256].astype(BF16)
            tails.append(increment[256:].reshape(16, 1, 8, WIDE))
        IS[h, 2] = jnp.concatenate(tails, axis=1).reshape(256, WIDE).astype(BF16)

        def send(i, carry):
            exchange(h, lax.rem(me + i, n), IS, IR, s2, r2).start()
            return carry

        lax.fori_loop(1, n, send, 0)
        IR[h, :, rows_of(me), :] = IS[h, :, rows_of(me), :]
        return carry

    lax.fori_loop(0, CHUNKS, network, 0)

    for h in range(CHUNKS):
        wgrad[:, h * WIDE : (h + 1) * WIDE] = WG[h]

    def collect(h, carry):
        all_of(h, IR, r2).wait()

        def add(p, carry):
            for k in range(PER):
                t = h * PER + k
                lanes = pl.ds(k * LANES, LANES)
                values = unpacked([IR[h, part, rows_of(p), lanes] for part in range(3)])
                for r in range(2):
                    rows = pl.ds(2 * p + r, DIRS, stride=RING)
                    D[t, rows, :] = C[t, rows, :] + values[r]
            return carry

        return lax.fori_loop(0, n, add, carry, unroll=4)

    lax.fori_loop(0, CHUNKS, collect, 0)
    for h in range(CHUNKS):
        all_of(h, S, s1).wait()
        all_of(h, IS, s2).wait()
    for side, there in sides:

        @pl.when(there)
        def _(side=side):
            for h in range(CHUNKS):
                halo_copy(h, side).wait_send()


def finish(total, slope, out, wgrad, out_sem, w_sem):
    def store(t):
        return pltpu.make_async_copy(
            total.at[t, :, pl.ds(0, ROWS), :], out.at[:, :, pl.ds(t * LANES, LANES)], out_sem.at[t]
        )

    copies = [store(t) for t in range(TILES)] + [pltpu.make_async_copy(slope, wgrad, w_sem)]
    for copy in copies:
        copy.start()
    for copy in copies:
        copy.wait()


def shards(n, slabs, forcing, state, wind, cg, turn, sea, sign, w_in, w_out, ww):
    angle = (np.arange(DIRS) + 0.5) * (2.0 * math.pi / DIRS)
    along = jnp.asarray(
        np.stack([0.5 * np.abs(np.cos(angle)), 0.5 * np.abs(np.sin(angle))]).astype(np.float32)
    )
    hbm = pl.BlockSpec(memory_space=pl.ANY)
    vmem = pl.BlockSpec(memory_space=pltpu.VMEM)
    smem = pl.BlockSpec(memory_space=pltpu.SMEM)
    sems = pltpu.SemaphoreType.DMA
    field = (TILES, DIRS, RING, LANES)
    fluxes = (TILES + 2, DIRS * RING, LANES)
    cells = (TILES, ROWS, LANES)
    message = (CHUNKS, 3, 16 * n, WIDE)
    total, slope = pl.pallas_call(
        functools.partial(kernel, n, slabs),
        out_shape=(
            pltpu.VMEM(field, F32),
            pltpu.VMEM(wind.shape, F32),
        ),
        in_specs=[hbm] * 9 + [smem] * 2,
        out_specs=(vmem, vmem),
        scratch_shapes=[
            pltpu.VMEM(field, F32),
            pltpu.VMEM(fluxes, F32),
            pltpu.VMEM(fluxes, F32),
            pltpu.VMEM(cells, F32),
            pltpu.VMEM(cells, F32),
            pltpu.VMEM(cells, F32),
            pltpu.VMEM(cells, F32),
            pltpu.VMEM((DIRS, LANES), F32),
            pltpu.VMEM((DIRS, LANES), F32),
            pltpu.VMEM((CHUNKS, 2, 3, 16, WIDE), BF16),
            pltpu.VMEM((CHUNKS, 2, 3, 16, WIDE), BF16),
            pltpu.VMEM(message, BF16),
            pltpu.VMEM(message, BF16),
            pltpu.VMEM(message, BF16),
            pltpu.VMEM(message, BF16),
            pltpu.VMEM((ROWS, TILES * LANES), jnp.int32),
            pltpu.VMEM((ROWS, TILES * LANES), jnp.int32),
            pltpu.VMEM((ROWS, TILES * LANES), jnp.int32),
            pltpu.VMEM(wind.shape, F32),
            pltpu.VMEM(ww.shape, F32),
            pltpu.VMEM((CHUNKS, COMPS, 2, WIDE), BF16),
            pltpu.VMEM(w_in.shape, BF16),
            pltpu.VMEM(w_out.shape, BF16),
            pltpu.VMEM((2, COMPS, 2 * COMPS), BF16),
            pltpu.VMEM((2, HID, 512), BF16),
            pltpu.VMEM((COMPS, HID), BF16),
            pltpu.VMEM((2, HID, WIDE), F32),
            pltpu.VMEM((HID, WIDE), BF16),
            pltpu.VMEM((HID, LANES), F32),
            pltpu.VMEM((CHUNKS, 2, WIDE), F32),
            sems((TILES,)),
            sems((7 + CHUNKS,)),
            sems((CHUNKS, 2)),
            sems((CHUNKS, 2)),
            sems((CHUNKS,)),
            sems((CHUNKS,)),
            sems((CHUNKS,)),
            sems((CHUNKS,)),
        ],
        compiler_params=pltpu.CompilerParams(
            collective_id=0, has_side_effects=True, vmem_limit_bytes=58 << 20
        ),
        name="adjoint_window",
    )(forcing, state, w_in, w_out, cg, turn, sea, wind, ww, sign, along)
    return pl.pallas_call(
        finish,
        out_shape=(
            jax.ShapeDtypeStruct(forcing.shape, F32),
            jax.ShapeDtypeStruct(wind.shape, F32),
        ),
        in_specs=[vmem] * 2,
        out_specs=(hbm, hbm),
        scratch_shapes=[sems((TILES,)), sems],
        compiler_params=pltpu.CompilerParams(vmem_limit_bytes=16 << 20),
        name="finish",
    )(total, slope)


def solution(mesh):
    placed = (
        P("comp", "space", None),
        P(None, ("space", "comp"), None),
        P(("space", "comp"), None),
        P("comp", "space", None),
        P("comp", "space", None),
        P("space", None),
        P(),
        P(),
        P(),
        P(),
    )
    return jax.shard_map(
        functools.partial(shards, mesh.shape["comp"], mesh.shape["space"]),
        mesh=mesh,
        in_specs=placed,
        out_specs=(P("comp", "space", None), P(("space", "comp"), None)),
        check_vma=False,
    )
```
